512 devices in a mesh: uly: 32 (over z_hi, x, core), blk: 16 (over y, z_lo).
Axes of the slice: x: 4, y: 8, z: 8 (z_hi: 4, z_lo: 2; z = z_hi * 2 + z_lo), core: 2. Of those that a mesh axis runs over, the one named last changes fastest.
Arguments:
- packed_queries: bfloat16 [65536, 4096], P(('blk', 'uly')), may hold values from -8 to 8
- packed_keys: bfloat16 [65536, 256], P(('blk', 'uly')), may hold values from -8 to 8
- packed_values: bfloat16 [65536, 256], P(('blk', 'uly')), may hold values from -6 to 6
- output_cotangent: bfloat16 [65536, 4096], P(('blk', 'uly')), may hold values from -6 to 6
- doc_offsets: int32 [130], replicated, may hold values from 0 to 65536, as said below
Outputs:
- attended: bfloat16 [65536, 4096], P(('blk', 'uly'))
- grad_queries: bfloat16 [65536, 4096], P(('blk', 'uly'))
- keys_gradient: bfloat16 [65536, 256], P(('blk', 'uly'))
- values_gradient: bfloat16 [65536, 256], P(('blk', 'uly'))
The draws below stay inside these ranges and needn't reach their ends.
Inputs may be any that keep to these rules, and one draw needn't show every extreme that they name: doc_offsets never fall; the first is 0 and the last 65536; each document, from one offset to the next, is 256 to 1024 tokens long and starts at a multiple of 128; some document is exactly 1024 long.
All inputs are finite; a program needn't handle non-finite values.
Results may differ from the reference program's by a relative error of at most 0.04.
Values may be sent and summed in bfloat16 or wider, within the bound.
No kernel may reach another device: no remote copies, remote signals or barrier semaphores. Data moves between devices by JAX's collectives and lax.ppermute only.
A program may use at most 64 MiB of HBM per device.

```python
import math
import jax
import jax.numpy as jnp
from jax import lax

QUERY_HEADS = 32
KEY_VALUE_HEADS = 2
HEAD_SIZE = 128
REGION = 4096
PACK_TOKENS = 65536
QUANT = 128
LONGEST_DOCUMENT = 1024


def draw_packed_queries(key, part):
    key = jax.random.fold_in(key, 8)
    return jnp.clip(jax.random.normal(key, (PACK_TOKENS, QUERY_HEADS * HEAD_SIZE), jnp.float32), -6.0, 6.0).astype(jnp.bfloat16)


def draw_packed_keys(key, part):
    key = jax.random.fold_in(key, 7)
    return jnp.clip(jax.random.normal(key, (PACK_TOKENS, KEY_VALUE_HEADS * HEAD_SIZE), jnp.float32), -6.0, 6.0).astype(jnp.bfloat16)


def draw_doc_offsets(key, part):
    key = jax.random.fold_in(key, 11)
    regions = PACK_TOKENS // REGION
    inner_cross = jax.random.randint(jax.random.fold_in(key, 1), (regions - 1,), 1, 8).astype(jnp.int32)
    four_q = jnp.full((1,), 4, jnp.int32)
    cross_left = jnp.concatenate([four_q, inner_cross, four_q])
    pair_cuts = jax.random.randint(jax.random.fold_in(key, 2), (regions, 2), 2, 5).astype(jnp.int32)
    lead_q = 8 - cross_left[:-1]
    trail_q = cross_left[1:]
    extra_q = 32 - lead_q - trail_q - 12
    third_q = extra_q // 3
    pair_base = lead_q[:, None] + 6 * jnp.arange(2, dtype=jnp.int32)[None, :]
    pair_starts = jnp.stack([pair_base, pair_base + pair_cuts], -1).reshape(regions, 4)
    rest_base = lead_q + 12
    rest_starts = jnp.stack([rest_base, rest_base + third_q, rest_base + 2 * third_q], -1)
    cross_start = (32 - trail_q)[:, None]
    starts = jnp.concatenate([pair_starts, rest_starts, cross_start], 1) + 32 * jnp.arange(regions, dtype=jnp.int32)[:, None]
    zero_start = jnp.zeros((1,), jnp.int32)
    ending = jnp.full((1,), 32 * regions, jnp.int32)
    return (jnp.concatenate([zero_start, starts.reshape(-1), ending]) * QUANT).astype(jnp.int32)


def level_of(stream_key, dims, split, smallest, largest):
    def one(position, parts):
        draws = jax.random.uniform(jax.random.fold_in(jax.random.fold_in(stream_key, 6), position), (parts,), jnp.float32, smallest / len(split), largest / len(split))
        return jnp.repeat(jnp.exp(draws), dims[position] // parts).reshape((-1,) + (1,) * (len(dims) - position - 1))

    level = one(*split[0])
    for cut in split[1:]:
        level = level * one(*cut)
    return level


def normal_values(stream_key, extent, scale, limit, shards=(), kind=jnp.bfloat16):
    array = jax.random.normal(stream_key, extent, jnp.float32) * scale
    if len(shards) > 0:
        array = level_of(stream_key, extent, shards, -0.22, 0.18) * array
    return jnp.clip(array, min=-limit, max=limit).astype(kind)


def setup_inputs(seed: int = 0) -> dict:
    splits = jax.random.split(jax.random.key(seed), 6)
    return {
        "packed_queries": draw_packed_queries(jax.random.fold_in(splits[5], 71), 0),
        "packed_keys": draw_packed_keys(jax.random.fold_in(splits[5], 71), 0),
        "packed_values": normal_values(splits[2], (PACK_TOKENS, KEY_VALUE_HEADS * HEAD_SIZE), 1.0, 6.0, ((0, 512),)),
        "output_cotangent": normal_values(splits[3], (PACK_TOKENS, QUERY_HEADS * HEAD_SIZE), 1.0, 6.0, ((0, 512),)),
        "doc_offsets": draw_doc_offsets(jax.random.fold_in(splits[5], 71), 0),
    }


def doc_starts(doc_offsets, positions):
    return lax.optimization_barrier(jnp.max(jnp.where(doc_offsets[None, :] <= positions[:, None], doc_offsets[None, :], 0), axis=1))

def allowed(query_pos, key_pos, starts):
    return (key_pos[None, :] <= query_pos[:, None]) & (key_pos[None, :] >= starts[:, None])

def attend_block(query_blk, key_win, value_win, visible, cot_blk, score_scale):
    query_wide = query_blk.astype(jnp.float32)
    key_wide = key_win.astype(jnp.float32)
    value_wide = value_win.astype(jnp.float32)
    cot_wide = cot_blk.astype(jnp.float32)
    scores = jnp.einsum('tcgd,wcd->cgtw', query_wide, key_wide) * score_scale
    scores = jnp.where(visible[None, None], scores, -jnp.inf)
    row_max = lax.optimization_barrier(jnp.max(scores, axis=-1, keepdims=True))
    row_sum = lax.optimization_barrier(jnp.sum(jnp.exp(scores - row_max), axis=-1, keepdims=True))
    log_total = row_max + jnp.log(row_sum)
    weights = jnp.exp(scores - log_total)
    weights_low = lax.optimization_barrier(weights.astype(jnp.bfloat16)).astype(jnp.float32)
    attended_b = jnp.einsum('cgtw,wcd->tcgd', weights_low, value_wide).astype(jnp.bfloat16)
    attended_wide = lax.optimization_barrier(attended_b).astype(jnp.float32)
    row_delta = jnp.einsum('tcgd,tcgd->cgt', cot_wide, attended_wide)
    value_grad = jnp.einsum('cgtw,tcgd->wcd', weights_low, cot_wide)
    grad_probs = jnp.einsum('tcgd,wcd->cgtw', cot_wide, value_wide)
    grad_scores = (weights * (grad_probs - row_delta[..., None])).astype(jnp.bfloat16)
    grad_scores = lax.optimization_barrier(grad_scores).astype(jnp.float32)
    query_grad = (jnp.einsum('cgtw,wcd->tcgd', grad_scores, key_wide) * score_scale).astype(jnp.bfloat16)
    key_grad = jnp.einsum('cgtw,tcgd->wcd', grad_scores, query_wide) * score_scale
    return (attended_b, query_grad, key_grad, value_grad)

def reference(packed_queries, packed_keys, packed_values, output_cotangent, doc_offsets):
    block_rows = min(128, REGION)
    window_rows = block_rows + LONGEST_DOCUMENT
    query_group_count = QUERY_HEADS // KEY_VALUE_HEADS
    score_scale = 1.0 / math.sqrt(HEAD_SIZE)
    queries_parted = packed_queries.reshape(PACK_TOKENS, KEY_VALUE_HEADS, query_group_count, HEAD_SIZE)
    cotangent_parted = output_cotangent.reshape(PACK_TOKENS, KEY_VALUE_HEADS, query_group_count, HEAD_SIZE)
    padded_keys = jnp.concatenate([jnp.zeros((LONGEST_DOCUMENT, KEY_VALUE_HEADS, HEAD_SIZE), packed_keys.dtype), packed_keys.reshape(PACK_TOKENS, KEY_VALUE_HEADS, HEAD_SIZE)], 0)
    padded_values = jnp.concatenate([jnp.zeros((LONGEST_DOCUMENT, KEY_VALUE_HEADS, HEAD_SIZE), packed_values.dtype), packed_values.reshape(PACK_TOKENS, KEY_VALUE_HEADS, HEAD_SIZE)], 0)

    def one_block(running, step_num):
        key_gradient_part, value_gradient_part = running
        row_start = (step_num * block_rows).astype(jnp.int32)
        query_blk = lax.dynamic_slice_in_dim(queries_parted, row_start, block_rows, 0)
        cot_blk = lax.dynamic_slice_in_dim(cotangent_parted, row_start, block_rows, 0)
        key_win = lax.dynamic_slice_in_dim(padded_keys, row_start, window_rows, 0)
        value_win = lax.dynamic_slice_in_dim(padded_values, row_start, window_rows, 0)
        query_pos = row_start + jnp.arange(block_rows, dtype=jnp.int32)
        key_pos = row_start - LONGEST_DOCUMENT + jnp.arange(window_rows, dtype=jnp.int32)
        visible = allowed(query_pos, key_pos, doc_starts(doc_offsets, query_pos))
        attended_b, query_grad, key_grad, value_grad = attend_block(query_blk, key_win, value_win, visible, cot_blk, score_scale)
        key_gradient_part = lax.dynamic_update_slice_in_dim(key_gradient_part, lax.dynamic_slice_in_dim(key_gradient_part, row_start, window_rows, 0) + key_grad, row_start, 0)
        value_gradient_part = lax.dynamic_update_slice_in_dim(value_gradient_part, lax.dynamic_slice_in_dim(value_gradient_part, row_start, window_rows, 0) + value_grad, row_start, 0)
        return ((key_gradient_part, value_gradient_part), (attended_b, query_grad))
    empty_gradients = jnp.zeros((PACK_TOKENS + LONGEST_DOCUMENT, KEY_VALUE_HEADS, HEAD_SIZE), jnp.float32)
    (key_gradient_part, value_gradient_part), (attended_all, query_all) = lax.scan(one_block, (empty_gradients, empty_gradients), jnp.arange(PACK_TOKENS // block_rows, dtype=jnp.int32))
    attended = attended_all.reshape(PACK_TOKENS, QUERY_HEADS * HEAD_SIZE)
    grad_queries = query_all.reshape(PACK_TOKENS, QUERY_HEADS * HEAD_SIZE)
    keys_gradient = key_gradient_part[LONGEST_DOCUMENT:].reshape(PACK_TOKENS, KEY_VALUE_HEADS * HEAD_SIZE).astype(jnp.bfloat16)
    values_gradient = value_gradient_part[LONGEST_DOCUMENT:].reshape(PACK_TOKENS, KEY_VALUE_HEADS * HEAD_SIZE).astype(jnp.bfloat16)
    return (attended, grad_queries, keys_gradient, values_gradient)
```

```python
import functools
import math

import jax
import jax.numpy as jnp
from jax import lax
from jax.experimental import pallas as pl
from jax.experimental.pallas import tpu as pltpu
from jax.sharding import PartitionSpec as P

HEAD = 128
TOK = 128
RING = 8
KEYS = RING * TOK
SCALE = 1.0 / math.sqrt(HEAD)
SCALE2 = SCALE * math.log2(math.e)
F32 = jnp.float32
BF16 = jnp.bfloat16
HEADS_PER_STEP = 4


def dot(a, b, ca, cb):
    return lax.dot_general(a, b, (((ca,), (cb,)), ((), ())), preferred_element_type=F32)


def attention_kernel(
    where_ref, q_ref, do_ref, k_ref, v_ref, o_ref, dq_ref, dk_ref, dv_ref, bias, dk_acc, dv_acc, *, steps
):
    step = pl.program_id(0)
    part = lax.rem(step, steps)

    @pl.when(step == 0)
    def _():
        position, before = where_ref[0], where_ref[1]
        row = lax.broadcasted_iota(jnp.int32, (TOK, TOK), 0)
        col = lax.broadcasted_iota(jnp.int32, (TOK, TOK), 1)
        for slot in range(RING):
            behind = lax.rem(position - slot + RING, RING)
            seen = ((behind == 0) & (col <= row)) | ((behind > 0) & (behind <= before))
            bias[:, slot * TOK : (slot + 1) * TOK] = jnp.where(seen, 0.0, -1e30).astype(F32)

    k, v = k_ref[...], v_ref[...]
    heads = HEADS_PER_STEP
    q = jnp.concatenate([q_ref[:, r * HEAD : (r + 1) * HEAD] for r in range(heads)], 0)
    do = jnp.concatenate([do_ref[:, r * HEAD : (r + 1) * HEAD] for r in range(heads)], 0)
    s = dot(q, k, 1, 1) + jnp.concatenate([bias[...]] * heads, 0)
    top = jnp.max(s, axis=1, keepdims=True)
    p = jnp.exp2(s * SCALE2 - top * SCALE2)
    inv = 1.0 / jnp.sum(p, axis=1, keepdims=True)
    p_low = p.astype(BF16)
    o = (dot(p_low, v, 1, 0) * inv).astype(BF16)
    do_wide = do.astype(F32)
    delta = jnp.sum(do_wide * o.astype(F32), axis=1, keepdims=True) * inv
    do_norm = (do_wide * inv).astype(BF16)
    ds = (p * (dot(do_norm, v, 1, 1) - delta)).astype(BF16)
    dq = (dot(ds, k, 1, 0) * SCALE).astype(BF16)
    for r in range(heads):
        o_ref[:, r * HEAD : (r + 1) * HEAD] = o[r * TOK : (r + 1) * TOK]
        dq_ref[:, r * HEAD : (r + 1) * HEAD] = dq[r * TOK : (r + 1) * TOK]
    dk = dot(q.T, ds, 1, 0)
    dv = dot(do_norm.T, p_low, 1, 0)

    @pl.when(part == 0)
    def _():
        dk_acc[...] = dk
        dv_acc[...] = dv

    @pl.when(part != 0)
    def _():
        dk_acc[...] += dk
        dv_acc[...] += dv

    @pl.when(part == steps - 1)
    def _():
        dk_ref[...] = (dk_acc[...] * SCALE).T.astype(BF16)
        dv_ref[...] = dv_acc[...].T.astype(BF16)


def attention(where, q, do, k, v):
    kv_heads = k.shape[1] // HEAD
    width = HEADS_PER_STEP * HEAD
    total = q.shape[1] // width
    steps = total // kv_heads
    rows = pl.BlockSpec((TOK, width), lambda i, w: (0, i))
    keys = pl.BlockSpec((KEYS, HEAD), lambda i, w: (0, i // steps))
    return pl.pallas_call(
        functools.partial(attention_kernel, steps=steps),
        grid_spec=pltpu.PrefetchScalarGridSpec(
            num_scalar_prefetch=1,
            grid=(total,),
            in_specs=[rows, rows, keys, keys],
            out_specs=[rows, rows, keys, keys],
            scratch_shapes=[
                pltpu.VMEM((TOK, KEYS), F32),
                pltpu.VMEM((HEAD, KEYS), F32),
                pltpu.VMEM((HEAD, KEYS), F32),
            ],
        ),
        out_shape=[jax.ShapeDtypeStruct(q.shape, BF16)] * 2 + [jax.ShapeDtypeStruct(k.shape, BF16)] * 2,
        compiler_params=pltpu.CompilerParams(
            vmem_limit_bytes=48 << 20, dimension_semantics=("arbitrary",)
        ),
        cost_estimate=pl.CostEstimate(
            flops=12 * TOK * KEYS * q.shape[1],
            bytes_accessed=8 * q.size + 8 * k.size,
            transcendentals=TOK * KEYS * q.shape[1] // HEAD,
        ),
    )(where, q, do, k, v)


def ring_shift(block, rings):
    lanes, regions = lax.axis_size("uly"), lax.axis_size("blk")
    tokens = lanes * regions

    def device(place):
        return (place % lanes) * regions + place // lanes

    route = [
        (device(i), device(i + rings * RING)) for i in range(tokens) if 0 <= i + rings * RING < tokens
    ]
    return lax.ppermute(block, ("uly", "blk"), route)


def within_ring(blocks):
    lanes = lax.axis_size("uly")
    groups = [list(range(r, r + RING)) for r in range(0, lanes, RING)]
    return lax.all_to_all(blocks, "uly", 0, 0, axis_index_groups=groups, tiled=True)


def shards(queries, keys, values, cotangent, doc_offsets):
    lane = lax.axis_index("uly")
    position = lane % RING
    first = (lax.axis_index("blk") * lax.axis_size("uly") + lane) * TOK
    start = jnp.max(jnp.where(doc_offsets <= first, doc_offsets, 0))
    where = jnp.stack([position, (first - start) // TOK]).astype(jnp.int32)
    slot = jnp.arange(RING)[:, None, None]

    own = jnp.concatenate([keys, values], 1)
    behind = ring_shift(own, 1)
    seen = within_ring(jnp.where(slot >= position, own[None], behind[None]))
    width = keys.shape[1]
    seen = seen.reshape(KEYS, 2 * width)
    attended, grad_q, grad_k, grad_v = attention(
        where, queries, cotangent, seen[:, :width], seen[:, width:]
    )
    terms = within_ring(jnp.concatenate([grad_k, grad_v], 1).reshape(RING, TOK, 2 * width)).astype(F32)
    mine = jnp.sum(jnp.where(slot >= position, terms, 0.0), 0)
    theirs = jnp.sum(jnp.where(slot >= position, 0.0, terms), 0).astype(BF16)
    total = (mine + ring_shift(theirs, -1).astype(F32)).astype(BF16)
    return attended, grad_q, total[:, :width], total[:, width:]


def solution(mesh):
    split = P(("blk", "uly"), None)
    return jax.shard_map(
        shards,
        mesh=mesh,
        in_specs=(split, split, split, split, P()),
        out_specs=(split, split, split, split),
        check_vma=False,
    )
```

```python
import math

import jax
import jax.numpy as jnp
from jax import lax
from jax.experimental import pallas as pl
from jax.experimental.pallas import tpu as pltpu
from jax.sharding import PartitionSpec as P

HEAD = 128
TOK = 128
RING = 8
KEYS = RING * TOK
SPAN = KEYS + TOK
SCALE = 1.0 / math.sqrt(HEAD)
SCALE2 = SCALE * math.log2(math.e)
F32 = jnp.float32
BF16 = jnp.bfloat16


def dot(a, b, ca, cb):
    return lax.dot_general(a, b, (((ca,), (cb,)), ((), ())), preferred_element_type=F32)


def stacked(ref):
    return jnp.concatenate([ref[:, r * HEAD : (r + 1) * HEAD] for r in range(ref.shape[1] // HEAD)], 0)


def attention_kernel(
    where_ref,
    offsets_ref,
    q_here_ref,
    do_here_ref,
    q_there_ref,
    do_there_ref,
    seen_ref,
    own_here_ref,
    own_there_ref,
    o_here_ref,
    dq_here_ref,
    there_ref,
    terms_ref,
    mine_here_ref,
    q_now,
    do_now,
    own_now,
    first_own,
    k_fill,
    k_zero,
    v_zero,
    o_now,
    dq_now,
    dk_acc,
    dv_acc,
):
    core, chip = where_ref[0], where_ref[1]
    side = pl.program_id(0)
    index = lax.rem(core + side, 2)
    half = q_now.shape[1]
    first_token = where_ref[2] + index * TOK
    offsets = offsets_ref[...]
    start = jnp.max(jnp.where(offsets <= first_token, offsets, 0))
    before = lax.shift_right_logical(first_token - start, 7)

    def slot(m):
        return lax.rem(2 * chip + 1 + m, RING)

    @pl.when(side == 0)
    def _():
        mine = pl.ds(pl.multiple_of(core * half, half), half)
        q_now[...] = q_here_ref[:, mine]
        do_now[...] = do_here_ref[:, mine]
        own_now[...] = own_here_ref[...]
        dk_acc[...] = jnp.zeros_like(dk_acc)
        dv_acc[...] = jnp.zeros_like(dv_acc)

    @pl.when(side == 1)
    def _():
        q_now[...] = q_there_ref[...]
        do_now[...] = do_there_ref[...]
        own_now[...] = own_there_ref[...]

    @pl.when(core == 0)
    def _():
        first_own[...] = own_here_ref[...]

    @pl.when(core == 1)
    def _():
        first_own[...] = own_there_ref[...]

    first = jnp.broadcast_to(own_now[0:1, :HEAD], (TOK, HEAD))
    zero = jnp.zeros((TOK, HEAD), BF16)
    for w in range(RING - 1):
        at = slice(w * TOK, (w + 1) * TOK)
        block = seen_ref[slot(w + index)]
        if w == RING - 2:
            block = jnp.where(index == 1, first_own[...], block)
        shown = RING - 1 - w <= before
        k_fill[at] = jnp.where(shown, block[:, :HEAD], first)
        k_zero[at] = jnp.where(shown, block[:, :HEAD], zero)
        v_zero[at] = jnp.where(shown, block[:, HEAD:], zero)
    last = slice(KEYS - TOK, KEYS)
    k_fill[last] = own_now[:, :HEAD]
    k_zero[last] = own_now[:, :HEAD]
    v_zero[last] = own_now[:, HEAD:]
    hidden = RING - 1 - before

    heads = half // HEAD
    q, do = stacked(q_now), stacked(do_now)
    k, v = k_fill[...], v_zero[...]
    row = lax.broadcasted_iota(jnp.int32, (TOK, TOK), 0)
    col = lax.broadcasted_iota(jnp.int32, (TOK, TOK), 1)
    causal = jnp.where(col <= row, 0.0, -1e30).astype(F32)
    s = dot(q, k, 1, 1)
    s = jnp.concatenate([s[:, : KEYS - TOK], s[:, KEYS - TOK :] + jnp.concatenate([causal] * heads, 0)], 1)
    top = jnp.max(s, axis=1, keepdims=True)
    p = jnp.exp2(s * SCALE2 - top * SCALE2)
    p_low = p.astype(BF16)
    wide = p[:, :TOK]
    for w in range(1, RING):
        wide = wide + p[:, w * TOK : (w + 1) * TOK]
    total = jnp.sum(wide - hidden.astype(F32) * p[:, :TOK], axis=1, keepdims=True)
    inv = 1.0 / total
    o = (dot(p_low, v, 1, 0) * inv).astype(BF16)
    do_wide = do.astype(F32)
    delta = jnp.sum(do_wide * o.astype(F32), axis=1, keepdims=True) * inv
    do_norm = (do_wide * inv).astype(BF16)
    ds = p_low * (dot(do_norm, v, 1, 1) - delta).astype(BF16)
    dq = (dot(ds, k_zero[...], 1, 0) * SCALE).astype(BF16)
    for r in range(heads):
        o_now[:, r * HEAD : (r + 1) * HEAD] = o[r * TOK : (r + 1) * TOK]
        dq_now[:, r * HEAD : (r + 1) * HEAD] = dq[r * TOK : (r + 1) * TOK]
    place = lax.broadcasted_iota(jnp.int32, (HEAD, KEYS), 1)
    shown = place >= hidden * TOK
    window = pl.ds(pl.multiple_of(index * TOK, TOK), KEYS)
    dk_acc[:, window] += jnp.where(shown, dot(q.T, ds, 1, 0), 0.0)
    dv_acc[:, window] += jnp.where(shown, dot(do_norm.T, p_low, 1, 0), 0.0)

    @pl.when(side == 0)
    def _():
        o_here_ref[...] = o_now[...]
        dq_here_ref[...] = dq_now[...]

    @pl.when(side == 1)
    def _():
        there_ref[:, :half] = o_now[...]
        there_ref[:, half : 2 * half] = dq_now[...]

        def block(m):
            cols = slice(m * TOK, (m + 1) * TOK)
            return (dk_acc[:, cols] * SCALE).T.astype(BF16), dv_acc[:, cols].T.astype(BF16)

        for m in range(RING - 1):
            terms_ref[slot(m), :, :HEAD], terms_ref[slot(m), :, HEAD:] = block(m)
        terms_ref[2 * chip] = jnp.zeros((TOK, 2 * HEAD), BF16)
        even_k, even_v = block(RING - 1)
        odd_k, odd_v = block(RING)
        swap = core == 1
        mine_here_ref[:, :HEAD] = jnp.where(swap, odd_k, even_k)
        mine_here_ref[:, HEAD:] = jnp.where(swap, odd_v, even_v)
        there_ref[:, 2 * half : 2 * half + HEAD] = jnp.where(swap, even_k, odd_k)
        there_ref[:, 2 * half + HEAD :] = jnp.where(swap, even_v, odd_v)


def attention(where, offsets, queries, cotangent, q_there, do_there, seen, own_here, own_there):
    half = q_there.shape
    rows = half[1] // HEAD * TOK
    own = own_here.shape
    there = (TOK, 2 * half[1] + own[1])
    vmem = pl.BlockSpec(memory_space=pltpu.VMEM)
    return pl.pallas_call(
        attention_kernel,
        grid_spec=pltpu.PrefetchScalarGridSpec(
            num_scalar_prefetch=1,
            grid=(2,),
            in_specs=[vmem] * 8,
            out_specs=[vmem] * 5,
            scratch_shapes=[
                pltpu.VMEM(half, BF16),
                pltpu.VMEM(half, BF16),
                pltpu.VMEM(own, BF16),
                pltpu.VMEM(own, BF16),
                pltpu.VMEM((KEYS, HEAD), BF16),
                pltpu.VMEM((KEYS, HEAD), BF16),
                pltpu.VMEM((KEYS, HEAD), BF16),
                pltpu.VMEM(half, BF16),
                pltpu.VMEM(half, BF16),
                pltpu.VMEM((HEAD, SPAN), F32),
                pltpu.VMEM((HEAD, SPAN), F32),
            ],
        ),
        out_shape=[
            jax.ShapeDtypeStruct(half, BF16),
            jax.ShapeDtypeStruct(half, BF16),
            jax.ShapeDtypeStruct(there, BF16),
            jax.ShapeDtypeStruct(seen.shape, BF16),
            jax.ShapeDtypeStruct(own, BF16),
        ],
        compiler_params=pltpu.CompilerParams(
            vmem_limit_bytes=44 << 20, dimension_semantics=("arbitrary",)
        ),
        cost_estimate=pl.CostEstimate(
            flops=24 * rows * KEYS * HEAD,
            bytes_accessed=16 * rows * HEAD,
            transcendentals=2 * rows * KEYS,
        ),
    )(where, offsets, queries, cotangent, q_there, do_there, seen, own_here, own_there)


def ring_shift(block, rings):
    lanes, regions = lax.axis_size("uly"), lax.axis_size("blk")
    tokens = lanes * regions

    def device(place):
        return (place % lanes) * regions + place // lanes

    route = [
        (device(i), device(i + rings * RING)) for i in range(tokens) if 0 <= i + rings * RING < tokens
    ]
    return lax.ppermute(block, ("uly", "blk"), route)


def within_ring(blocks):
    lanes = lax.axis_size("uly")
    groups = [list(range(r, r + RING)) for r in range(0, lanes, RING)]
    return lax.all_to_all(blocks, "uly", 0, 0, axis_index_groups=groups, tiled=True)


def to_sibling(block):
    lanes = lax.axis_size("uly")
    return lax.ppermute(block, "uly", [(i, i ^ 1) for i in range(lanes)])


def to_sibling(block):
    lanes = lax.axis_size("uly")
    return lax.ppermute(block, "uly", [(i, i ^ 1) for i in range(lanes)])


def shards(queries, keys, values, cotangent, doc_offsets):
    lane = lax.axis_index("uly")
    core, chip = lane & 1, (lane >> 1) & (RING // 2 - 1)
    first = (lax.axis_index("blk") * lax.axis_size("uly") + lane - core) * TOK
    where = jnp.stack([core, chip, first]).astype(jnp.int32)
    slot_chip = (jnp.arange(RING) // 2)[:, None, None]

    def heads_of(block, group):
        width = block.shape[1] // 2
        return lax.dynamic_slice_in_dim(block, group * width, width, 1)

    def by_slot(block):
        return jnp.broadcast_to(
            block.reshape(1, TOK, 2, 2 * HEAD).transpose(0, 2, 1, 3), (RING // 2, 2, TOK, 2 * HEAD)
        ).reshape(RING, TOK, 2 * HEAD)

    kv = jnp.concatenate([keys[:, :HEAD], values[:, :HEAD], keys[:, HEAD:], values[:, HEAD:]], 1)
    behind = ring_shift(kv, 1)
    send = jnp.where(slot_chip > chip, by_slot(kv), by_slot(behind))
    halves = [heads_of(a, 1 - core) for a in (queries, cotangent, kv)]
    where, *halves = lax.optimization_barrier((where, *halves))
    seen = within_ring(send)
    q_there, do_there, own_there = [to_sibling(a) for a in halves]
    offsets = doc_offsets.reshape(1, -1)
    o_here, dq_here, there, terms, mine_here = attention(
        where, offsets, queries, cotangent, q_there, do_there, seen, heads_of(kv, core), own_there
    )

    terms = within_ring(terms).reshape(RING // 2, 2, TOK, 2 * HEAD)

    def picked(after):
        return sum(
            jnp.where((j > chip) == after, terms[j], jnp.zeros_like(terms[j])).astype(F32)
            for j in range(RING // 2)
        )

    shifted = ring_shift(picked(False).astype(BF16), -1)
    back = to_sibling(there)
    half = o_here.shape[1]

    def joined(a, b):
        return jnp.where(core == 0, jnp.concatenate([a, b], 1), jnp.concatenate([b, a], 1))

    attended, grad_q = joined(o_here, back[:, :half]), joined(dq_here, back[:, half : 2 * half])
    local = jnp.where(
        core == 0,
        jnp.stack([mine_here, back[:, 2 * half :]]),
        jnp.stack([back[:, 2 * half :], mine_here]),
    )
    ours = picked(True) + local.astype(F32)
    ours, attended, grad_q = lax.optimization_barrier((ours, attended, grad_q))
    total = (ours + shifted.astype(F32)).astype(BF16)
    grad_k = jnp.concatenate([total[0, :, :HEAD], total[1, :, :HEAD]], 1)
    grad_v = jnp.concatenate([total[0, :, HEAD:], total[1, :, HEAD:]], 1)
    return attended, grad_q, grad_k, grad_v


def solution(mesh):
    split = P(("blk", "uly"), None)
    return jax.shard_map(
        shards,
        mesh=mesh,
        in_specs=(split, split, split, split, P()),
        out_specs=(split, split, split, split),
        check_vma=False,
    )
```

```python
import functools
import math

import jax
import jax.numpy as jnp
from jax import lax
from jax.experimental import pallas as pl
from jax.experimental.pallas import tpu as pltpu
from jax.sharding import PartitionSpec as P

HEAD = 128
TOK = 128
RING = 8
KEYS = RING * TOK
SPAN = KEYS + TOK
SCALE = 1.0 / math.sqrt(HEAD)
SCALE2 = SCALE * math.log2(math.e)
F32 = jnp.float32
BF16 = jnp.bfloat16


def dot(a, b, ca, cb):
    return lax.dot_general(a, b, (((ca,), (cb,)), ((), ())), preferred_element_type=F32)


def stacked(ref):
    return jnp.concatenate([ref[:, r * HEAD : (r + 1) * HEAD] for r in range(ref.shape[1] // HEAD)], 0)


def attention_kernel(
    where_ref,
    offsets_ref,
    q_here_ref,
    do_here_ref,
    q_there_ref,
    do_there_ref,
    seen_ref,
    own_here_ref,
    own_there_ref,
    o_here_ref,
    dq_here_ref,
    there_ref,
    terms_ref,
    mine_here_ref,
    q_side,
    do_side,
    own_now,
    first_own,
    k_fill,
    k_zero,
    v_zero,
    o_now,
    dq_now,
    dk_acc,
    dv_acc,
    sems,
):
    core, chip = where_ref[0], where_ref[1]
    side = pl.program_id(0)
    index = lax.rem(core + side, 2)
    half = o_now.shape[1]
    first_token = where_ref[2] + index * TOK
    offsets = offsets_ref[...]
    start = jnp.max(jnp.where(offsets <= first_token, offsets, 0))
    before = lax.shift_right_logical(first_token - start, 7)

    def slot(m):
        return lax.rem(2 * chip + 1 + m, RING)

    mine = pl.ds(pl.multiple_of(core * half, half), half)
    fetches = [
        [
            pltpu.make_async_copy(q_here_ref.at[:, mine], q_side.at[0], sems.at[0]),
            pltpu.make_async_copy(do_here_ref.at[:, mine], do_side.at[0], sems.at[1]),
        ],
        [
            pltpu.make_async_copy(q_there_ref, q_side.at[1], sems.at[2]),
            pltpu.make_async_copy(do_there_ref, do_side.at[1], sems.at[3]),
        ],
    ]

    @pl.when(side == 0)
    def _():
        for fetch in fetches[0] + fetches[1]:
            fetch.start()
        own_now[...] = own_here_ref[...]
        dk_acc[...] = jnp.zeros_like(dk_acc)
        dv_acc[...] = jnp.zeros_like(dv_acc)

    @pl.when(side == 1)
    def _():
        own_now[...] = own_there_ref[...]

    @pl.when(core == 0)
    def _():
        first_own[...] = own_here_ref[...]

    @pl.when(core == 1)
    def _():
        first_own[...] = own_there_ref[...]

    first = jnp.broadcast_to(own_now[0:1, :HEAD], (TOK, HEAD))
    zero = jnp.zeros((TOK, HEAD), BF16)
    for w in range(RING - 1):
        at = slice(w * TOK, (w + 1) * TOK)
        block = seen_ref[slot(w + index)]
        if w == RING - 2:
            block = jnp.where(index == 1, first_own[...], block)
        shown = RING - 1 - w <= before
        k_fill[at] = jnp.where(shown, block[:, :HEAD], first)
        k_zero[at] = jnp.where(shown, block[:, :HEAD], zero)
        v_zero[at] = jnp.where(shown, block[:, HEAD:], zero)
    last = slice(KEYS - TOK, KEYS)
    k_fill[last] = own_now[:, :HEAD]
    k_zero[last] = own_now[:, :HEAD]
    v_zero[last] = own_now[:, HEAD:]

    @pl.when(side == 0)
    def _():
        for fetch in fetches[0]:
            fetch.wait()

    @pl.when(side == 1)
    def _():
        for fetch in fetches[1]:
            fetch.wait()

    def attend(tiles):
        width = 2 * tiles * TOK
        heads = half // HEAD
        q, do = stacked(q_side.at[side]), stacked(do_side.at[side])
        k, v = k_fill[KEYS - width :], v_zero[KEYS - width :]
        hidden = 2 * tiles - 1 - before
        row = lax.broadcasted_iota(jnp.int32, (TOK, TOK), 0)
        col = lax.broadcasted_iota(jnp.int32, (TOK, TOK), 1)
        causal = jnp.where(col <= row, 0.0, -1e30).astype(F32)
        s = dot(q, k, 1, 1)
        s = jnp.concatenate(
            [s[:, : width - TOK], s[:, width - TOK :] + jnp.concatenate([causal] * heads, 0)], 1
        )
        top = jnp.max(s, axis=1, keepdims=True)
        p = jnp.exp2(s * SCALE2 - top * SCALE2)
        p_low = p.astype(BF16)
        wide = p[:, :TOK]
        for w in range(1, 2 * tiles):
            wide = wide + p[:, w * TOK : (w + 1) * TOK]
        total = jnp.sum(wide - hidden.astype(F32) * p[:, :TOK], axis=1, keepdims=True)
        inv = 1.0 / total
        o = (dot(p_low, v, 1, 0) * inv).astype(BF16)
        do_wide = do.astype(F32)
        delta = jnp.sum(do_wide * o.astype(F32), axis=1, keepdims=True) * inv
        do_norm = (do_wide * inv).astype(BF16)
        ds = p_low * (dot(do_norm, v, 1, 1) - delta).astype(BF16)
        dq = (dot(ds, k_zero[KEYS - width :], 1, 0) * SCALE).astype(BF16)
        for r in range(heads):
            o_now[:, r * HEAD : (r + 1) * HEAD] = o[r * TOK : (r + 1) * TOK]
            dq_now[:, r * HEAD : (r + 1) * HEAD] = dq[r * TOK : (r + 1) * TOK]
        place = lax.broadcasted_iota(jnp.int32, (HEAD, width), 1)
        shown = place >= hidden * TOK
        window = pl.ds(pl.multiple_of(index * TOK + KEYS - width, TOK), width)
        dk_acc[:, window] += jnp.where(shown, dot(q.T, ds, 1, 0), 0.0)
        dv_acc[:, window] += jnp.where(shown, dot(do_norm.T, p_low, 1, 0), 0.0)

    for tiles in range(1, RING // 2 + 1):
        pl.when(lax.shift_right_logical(before, 1) == tiles - 1)(functools.partial(attend, tiles))

    @pl.when(side == 0)
    def _():
        o_here_ref[...] = o_now[...]
        dq_here_ref[...] = dq_now[...]

    @pl.when(side == 1)
    def _():
        there_ref[:, :half] = o_now[...]
        there_ref[:, half : 2 * half] = dq_now[...]

        def block(m):
            cols = slice(m * TOK, (m + 1) * TOK)
            return (dk_acc[:, cols] * SCALE).T.astype(BF16), dv_acc[:, cols].T.astype(BF16)

        for m in range(RING - 1):
            terms_ref[slot(m), :, :HEAD], terms_ref[slot(m), :, HEAD:] = block(m)
        terms_ref[2 * chip] = jnp.zeros((TOK, 2 * HEAD), BF16)
        even_k, even_v = block(RING - 1)
        odd_k, odd_v = block(RING)
        swap = core == 1
        mine_here_ref[:, :HEAD] = jnp.where(swap, odd_k, even_k)
        mine_here_ref[:, HEAD:] = jnp.where(swap, odd_v, even_v)
        there_ref[:, 2 * half : 2 * half + HEAD] = jnp.where(swap, even_k, odd_k)
        there_ref[:, 2 * half + HEAD :] = jnp.where(swap, even_v, odd_v)


def attention(where, offsets, queries, cotangent, q_there, do_there, seen, own_here, own_there):
    half = q_there.shape
    rows = half[1] // HEAD * TOK
    own = own_here.shape
    there = (TOK, 2 * half[1] + own[1])
    vmem = pl.BlockSpec(memory_space=pltpu.VMEM)
    anywhere = pl.BlockSpec(memory_space=pl.ANY)
    return pl.pallas_call(
        attention_kernel,
        grid_spec=pltpu.PrefetchScalarGridSpec(
            num_scalar_prefetch=1,
            grid=(2,),
            in_specs=[vmem] + [anywhere] * 4 + [vmem] * 3,
            out_specs=[vmem] * 5,
            scratch_shapes=[
                pltpu.VMEM((2, *half), BF16),
                pltpu.VMEM((2, *half), BF16),
                pltpu.VMEM(own, BF16),
                pltpu.VMEM(own, BF16),
                pltpu.VMEM((KEYS, HEAD), BF16),
                pltpu.VMEM((KEYS, HEAD), BF16),
                pltpu.VMEM((KEYS, HEAD), BF16),
                pltpu.VMEM(half, BF16),
                pltpu.VMEM(half, BF16),
                pltpu.VMEM((HEAD, SPAN), F32),
                pltpu.VMEM((HEAD, SPAN), F32),
                pltpu.SemaphoreType.DMA((4,)),
            ],
        ),
        out_shape=[
            jax.ShapeDtypeStruct(half, BF16),
            jax.ShapeDtypeStruct(half, BF16),
            jax.ShapeDtypeStruct(there, BF16),
            jax.ShapeDtypeStruct(seen.shape, BF16),
            jax.ShapeDtypeStruct(own, BF16),
        ],
        compiler_params=pltpu.CompilerParams(
            vmem_limit_bytes=44 << 20, dimension_semantics=("arbitrary",)
        ),
        cost_estimate=pl.CostEstimate(
            flops=24 * rows * KEYS * HEAD,
            bytes_accessed=16 * rows * HEAD,
            transcendentals=2 * rows * KEYS,
        ),
    )(where, offsets, queries, cotangent, q_there, do_there, seen, own_here, own_there)


def ring_shift(block, rings):
    lanes, regions = lax.axis_size("uly"), lax.axis_size("blk")
    tokens = lanes * regions

    def device(place):
        return (place % lanes) * regions + place // lanes

    route = [
        (device(i), device(i + rings * RING)) for i in range(tokens) if 0 <= i + rings * RING < tokens
    ]
    return lax.ppermute(block, ("uly", "blk"), route)


def within_ring(blocks):
    lanes = lax.axis_size("uly")
    groups = [list(range(r, r + RING)) for r in range(0, lanes, RING)]
    return lax.all_to_all(blocks, "uly", 0, 0, axis_index_groups=groups, tiled=True)


def to_sibling(block):
    lanes = lax.axis_size("uly")
    return lax.ppermute(block, "uly", [(i, i ^ 1) for i in range(lanes)])


def to_sibling(block):
    lanes = lax.axis_size("uly")
    return lax.ppermute(block, "uly", [(i, i ^ 1) for i in range(lanes)])


def shards(queries, keys, values, cotangent, doc_offsets):
    lane = lax.axis_index("uly")
    core, chip = lane & 1, (lane >> 1) & (RING // 2 - 1)
    first = (lax.axis_index("blk") * lax.axis_size("uly") + lane - core) * TOK
    where = jnp.stack([core, chip, first]).astype(jnp.int32)
    slot_chip = (jnp.arange(RING) // 2)[:, None, None]

    def heads_of(block, group):
        width = block.shape[1] // 2
        return lax.dynamic_slice_in_dim(block, group * width, width, 1)

    def by_slot(block):
        return jnp.broadcast_to(
            block.reshape(1, TOK, 2, 2 * HEAD).transpose(0, 2, 1, 3), (RING // 2, 2, TOK, 2 * HEAD)
        ).reshape(RING, TOK, 2 * HEAD)

    kv = jnp.concatenate([keys[:, :HEAD], values[:, :HEAD], keys[:, HEAD:], values[:, HEAD:]], 1)
    behind = ring_shift(kv, 1)
    send = jnp.where(slot_chip > chip, by_slot(kv), by_slot(behind))
    halves = [heads_of(a, 1 - core) for a in (queries, cotangent, kv)]
    where, *halves = lax.optimization_barrier((where, *halves))
    seen = within_ring(send)
    q_there, do_there, own_there = [to_sibling(a) for a in halves]
    offsets = doc_offsets.reshape(1, -1)
    o_here, dq_here, there, terms, mine_here = attention(
        where, offsets, queries, cotangent, q_there, do_there, seen, heads_of(kv, core), own_there
    )

    terms = within_ring(terms).reshape(RING // 2, 2, TOK, 2 * HEAD)

    def picked(after):
        return sum(
            jnp.where((j > chip) == after, terms[j], jnp.zeros_like(terms[j])).astype(F32)
            for j in range(RING // 2)
        )

    def side_by_side(a):
        return jnp.concatenate([a[0, :, :HEAD], a[1, :, :HEAD], a[0, :, HEAD:], a[1, :, HEAD:]], 1)

    shifted = ring_shift(side_by_side(picked(False).astype(BF16)), -1)
    back = to_sibling(there)
    half = o_here.shape[1]

    def joined(a, b):
        return jnp.where(core == 0, jnp.concatenate([a, b], 1), jnp.concatenate([b, a], 1))

    attended, grad_q = joined(o_here, back[:, :half]), joined(dq_here, back[:, half : 2 * half])
    local = jnp.where(
        core == 0,
        jnp.stack([mine_here, back[:, 2 * half :]]),
        jnp.stack([back[:, 2 * half :], mine_here]),
    )
    ours = side_by_side(picked(True) + local.astype(F32))
    ours, attended, grad_q = lax.optimization_barrier((ours, attended, grad_q))
    total = (ours + shifted.astype(F32)).astype(BF16)
    return attended, grad_q, total[:, : 2 * HEAD], total[:, 2 * HEAD :]


def solution(mesh):
    split = P(("blk", "uly"), None)
    return jax.shard_map(
        shards,
        mesh=mesh,
        in_specs=(split, split, split, split, P()),
        out_specs=(split, split, split, split),
        check_vma=False,
    )
```

```python
import functools
import math

import jax
import jax.numpy as jnp
from jax import lax
from jax.experimental import pallas as pl
from jax.experimental.pallas import tpu as pltpu
from jax.sharding import PartitionSpec as P

HEAD = 128
TOK = 128
RING = 8
KEYS = RING * TOK
SPAN = KEYS + TOK
SCALE = 1.0 / math.sqrt(HEAD)
SCALE2 = SCALE * math.log2(math.e)
F32 = jnp.float32
BF16 = jnp.bfloat16


def dot(a, b, ca, cb):
    return lax.dot_general(a, b, (((ca,), (cb,)), ((), ())), preferred_element_type=F32)


def stacked(ref):
    return jnp.concatenate([ref[:, r * HEAD : (r + 1) * HEAD] for r in range(ref.shape[1] // HEAD)], 0)


def attention_kernel(
    where_ref,
    offsets_ref,
    q_here_ref,
    do_here_ref,
    q_there_ref,
    do_there_ref,
    seen_ref,
    own_here_ref,
    own_there_ref,
    o_here_ref,
    dq_here_ref,
    there_ref,
    terms_ref,
    mine_here_ref,
    q_side,
    do_side,
    own_now,
    first_own,
    k_fill,
    k_zero,
    v_zero,
    o_now,
    dq_now,
    dk_acc,
    dv_acc,
    sems,
):
    core, chip = where_ref[0], where_ref[1]
    side = pl.program_id(0)
    index = lax.rem(core + side, 2)
    half = o_now.shape[1]
    first_token = where_ref[2] + index * TOK
    offsets = offsets_ref[...]
    start = jnp.max(jnp.where(offsets <= first_token, offsets, 0))
    before = lax.shift_right_logical(first_token - start, 7)

    def slot(m):
        return lax.rem(2 * chip + 1 + m, RING)

    mine = pl.ds(pl.multiple_of(core * half, half), half)
    fetches = [
        [
            pltpu.make_async_copy(q_here_ref.at[:, mine], q_side.at[0], sems.at[0]),
            pltpu.make_async_copy(do_here_ref.at[:, mine], do_side.at[0], sems.at[1]),
        ],
        [
            pltpu.make_async_copy(q_there_ref, q_side.at[1], sems.at[2]),
            pltpu.make_async_copy(do_there_ref, do_side.at[1], sems.at[3]),
        ],
    ]

    @pl.when(side == 0)
    def _():
        for fetch in fetches[0] + fetches[1]:
            fetch.start()
        own_now[...] = own_here_ref[...]
        dk_acc[...] = jnp.zeros_like(dk_acc)
        dv_acc[...] = jnp.zeros_like(dv_acc)

    @pl.when(side == 1)
    def _():
        own_now[...] = own_there_ref[...]

    @pl.when(core == 0)
    def _():
        first_own[...] = own_here_ref[...]

    @pl.when(core == 1)
    def _():
        first_own[...] = own_there_ref[...]

    first = jnp.broadcast_to(own_now[0:1, :HEAD], (TOK, HEAD))
    zero = jnp.zeros((TOK, HEAD), BF16)
    for w in range(RING - 1):
        at = slice(w * TOK, (w + 1) * TOK)
        block = seen_ref[slot(w + index)]
        if w == RING - 2:
            block = jnp.where(index == 1, first_own[...], block)
        shown = RING - 1 - w <= before
        k_fill[at] = jnp.where(shown, block[:, :HEAD], first)
        k_zero[at] = jnp.where(shown, block[:, :HEAD], zero)
        v_zero[at] = jnp.where(shown, block[:, HEAD:], zero)
    last = slice(KEYS - TOK, KEYS)
    k_fill[last] = own_now[:, :HEAD]
    k_zero[last] = own_now[:, :HEAD]
    v_zero[last] = own_now[:, HEAD:]

    @pl.when(side == 0)
    def _():
        for fetch in fetches[0]:
            fetch.wait()

    @pl.when(side == 1)
    def _():
        for fetch in fetches[1]:
            fetch.wait()

    def attend(tiles):
        width = 2 * tiles * TOK
        heads = half // HEAD
        hidden = 2 * tiles - 1 - before
        row = lax.broadcasted_iota(jnp.int32, (TOK, TOK), 0)
        col = lax.broadcasted_iota(jnp.int32, (TOK, TOK), 1)
        causal = jnp.where(col <= row, 0.0, -1e30).astype(F32)
        k, kz, v = k_fill[KEYS - width :], k_zero[KEYS - width :], v_zero[KEYS - width :]
        group_size = 8
        groups = range(0, heads, group_size)

        def part(ref, g):
            at = ref.at[side]
            return jnp.concatenate([at[:, (g + r) * HEAD : (g + r + 1) * HEAD] for r in range(group_size)], 0)

        qs = [part(q_side, g) for g in groups]
        scores = [dot(q, k, 1, 1) for q in qs]
        dss, ps, norms = [], [], []
        for g, s in zip(groups, scores):
            do = part(do_side, g)
            s = jnp.concatenate(
                [s[:, : width - TOK], s[:, width - TOK :] + jnp.concatenate([causal] * group_size, 0)], 1
            )
            top = jnp.max(s, axis=1, keepdims=True)
            p = jnp.exp2(s * SCALE2 - top * SCALE2)
            p_low = p.astype(BF16)
            wide = p[:, :TOK]
            for w in range(1, 2 * tiles):
                wide = wide + p[:, w * TOK : (w + 1) * TOK]
            total = jnp.sum(wide - hidden.astype(F32) * p[:, :TOK], axis=1, keepdims=True)
            inv = 1.0 / total
            o = (dot(p_low, v, 1, 0) * inv).astype(BF16)
            do_wide = do.astype(F32)
            delta = jnp.sum(do_wide * o.astype(F32), axis=1, keepdims=True) * inv
            do_norm = (do_wide * inv).astype(BF16)
            ds = p_low * (dot(do_norm, v, 1, 1) - delta).astype(BF16)
            dq = (dot(ds, kz, 1, 0) * SCALE).astype(BF16)
            for r in range(group_size):
                at = slice((g + r) * HEAD, (g + r + 1) * HEAD)
                o_now[:, at] = o[r * TOK : (r + 1) * TOK]
                dq_now[:, at] = dq[r * TOK : (r + 1) * TOK]
            dss.append(ds)
            ps.append(p_low)
            norms.append(do_norm)
        ds, p_low, do_norm, q = [jnp.concatenate(x, 0) for x in (dss, ps, norms, qs)]
        place = lax.broadcasted_iota(jnp.int32, (HEAD, width), 1)
        shown = place >= hidden * TOK
        window = pl.ds(pl.multiple_of(index * TOK + KEYS - width, TOK), width)
        dk_acc[:, window] += jnp.where(shown, dot(q.T, ds, 1, 0), 0.0)
        dv_acc[:, window] += jnp.where(shown, dot(do_norm.T, p_low, 1, 0), 0.0)

    for tiles in range(1, RING // 2 + 1):
        pl.when(lax.shift_right_logical(before, 1) == tiles - 1)(functools.partial(attend, tiles))

    @pl.when(side == 0)
    def _():
        o_here_ref[...] = o_now[...]
        dq_here_ref[...] = dq_now[...]

    @pl.when(side == 1)
    def _():
        there_ref[:, :half] = o_now[...]
        there_ref[:, half : 2 * half] = dq_now[...]

        def block(m):
            cols = slice(m * TOK, (m + 1) * TOK)
            return (dk_acc[:, cols] * SCALE).T.astype(BF16), dv_acc[:, cols].T.astype(BF16)

        for m in range(RING - 1):
            terms_ref[slot(m), :, :HEAD], terms_ref[slot(m), :, HEAD:] = block(m)
        terms_ref[2 * chip] = jnp.zeros((TOK, 2 * HEAD), BF16)
        even_k, even_v = block(RING - 1)
        odd_k, odd_v = block(RING)
        swap = core == 1
        mine_here_ref[:, :HEAD] = jnp.where(swap, odd_k, even_k)
        mine_here_ref[:, HEAD:] = jnp.where(swap, odd_v, even_v)
        there_ref[:, 2 * half : 2 * half + HEAD] = jnp.where(swap, even_k, odd_k)
        there_ref[:, 2 * half + HEAD :] = jnp.where(swap, even_v, odd_v)


def attention(where, offsets, queries, cotangent, q_there, do_there, seen, own_here, own_there):
    half = q_there.shape
    rows = half[1] // HEAD * TOK
    own = own_here.shape
    there = (TOK, 2 * half[1] + own[1])
    vmem = pl.BlockSpec(memory_space=pltpu.VMEM)
    anywhere = pl.BlockSpec(memory_space=pltpu.HBM)
    return pl.pallas_call(
        attention_kernel,
        grid_spec=pltpu.PrefetchScalarGridSpec(
            num_scalar_prefetch=1,
            grid=(2,),
            in_specs=[vmem] + [anywhere] * 4 + [vmem] * 3,
            out_specs=[vmem] * 5,
            scratch_shapes=[
                pltpu.VMEM((2, *half), BF16),
                pltpu.VMEM((2, *half), BF16),
                pltpu.VMEM(own, BF16),
                pltpu.VMEM(own, BF16),
                pltpu.VMEM((KEYS, HEAD), BF16),
                pltpu.VMEM((KEYS, HEAD), BF16),
                pltpu.VMEM((KEYS, HEAD), BF16),
                pltpu.VMEM(half, BF16),
                pltpu.VMEM(half, BF16),
                pltpu.VMEM((HEAD, SPAN), F32),
                pltpu.VMEM((HEAD, SPAN), F32),
                pltpu.SemaphoreType.DMA((4,)),
            ],
        ),
        out_shape=[
            jax.ShapeDtypeStruct(half, BF16),
            jax.ShapeDtypeStruct(half, BF16),
            jax.ShapeDtypeStruct(there, BF16),
            jax.ShapeDtypeStruct(seen.shape, BF16),
            jax.ShapeDtypeStruct(own, BF16),
        ],
        compiler_params=pltpu.CompilerParams(
            vmem_limit_bytes=44 << 20, dimension_semantics=("arbitrary",)
        ),
        cost_estimate=pl.CostEstimate(
            flops=24 * rows * KEYS * HEAD,
            bytes_accessed=16 * rows * HEAD,
            transcendentals=2 * rows * KEYS,
        ),
    )(where, offsets, queries, cotangent, q_there, do_there, seen, own_here, own_there)


def theirs_kernel(where_ref, terms_ref, out_ref):
    chip = where_ref[1]
    for group in range(2):
        total = terms_ref[group].astype(F32)
        for j in range(1, RING // 2):
            total += jnp.where(j > chip, 0.0, terms_ref[2 * j + group].astype(F32))
        k_at, v_at = group * HEAD, (2 + group) * HEAD
        out_ref[:, k_at : k_at + HEAD] = total[:, :HEAD].astype(BF16)
        out_ref[:, v_at : v_at + HEAD] = total[:, HEAD:].astype(BF16)


def theirs_sum(where, terms):
    vmem = pl.BlockSpec(memory_space=pltpu.VMEM)
    return pl.pallas_call(
        theirs_kernel,
        grid_spec=pltpu.PrefetchScalarGridSpec(
            num_scalar_prefetch=1, grid=(1,), in_specs=[vmem], out_specs=vmem
        ),
        out_shape=jax.ShapeDtypeStruct((TOK, 4 * HEAD), BF16),
        cost_estimate=pl.CostEstimate(flops=40_000_000_000, bytes_accessed=terms.size * 2, transcendentals=0),
    )(where, terms)


def ring_shift(block, rings):
    lanes, regions = lax.axis_size("uly"), lax.axis_size("blk")
    tokens = lanes * regions

    def device(place):
        return (place % lanes) * regions + place // lanes

    route = [
        (device(i), device(i + rings * RING)) for i in range(tokens) if 0 <= i + rings * RING < tokens
    ]
    return lax.ppermute(block, ("uly", "blk"), route)


def within_ring(blocks):
    lanes = lax.axis_size("uly")
    groups = [list(range(r, r + RING)) for r in range(0, lanes, RING)]
    return lax.all_to_all(blocks, "uly", 0, 0, axis_index_groups=groups, tiled=True)


def to_sibling(block):
    lanes = lax.axis_size("uly")
    return lax.ppermute(block, "uly", [(i, i ^ 1) for i in range(lanes)])


def to_sibling(block):
    lanes = lax.axis_size("uly")
    return lax.ppermute(block, "uly", [(i, i ^ 1) for i in range(lanes)])


def shards(queries, keys, values, cotangent, doc_offsets):
    lane = lax.axis_index("uly")
    core, chip = lane & 1, (lane >> 1) & (RING // 2 - 1)
    first = (lax.axis_index("blk") * lax.axis_size("uly") + lane - core) * TOK
    where = jnp.stack([core, chip, first]).astype(jnp.int32)
    slot_chip = (jnp.arange(RING) // 2)[:, None, None]

    def heads_of(block, group):
        width = block.shape[1] // 2
        return lax.dynamic_slice_in_dim(block, group * width, width, 1)

    def by_slot(block):
        return jnp.broadcast_to(
            block.reshape(1, TOK, 2, 2 * HEAD).transpose(0, 2, 1, 3), (RING // 2, 2, TOK, 2 * HEAD)
        ).reshape(RING, TOK, 2 * HEAD)

    kv = jnp.concatenate([keys[:, :HEAD], values[:, :HEAD], keys[:, HEAD:], values[:, HEAD:]], 1)
    behind = ring_shift(kv, 1)
    send = jnp.where(slot_chip > chip, by_slot(kv), by_slot(behind))
    halves = [heads_of(a, 1 - core) for a in (queries, cotangent, kv)]
    where, *halves = lax.optimization_barrier((where, *halves))
    seen = within_ring(send)
    q_there, do_there, own_there = [to_sibling(a) for a in halves]
    offsets = doc_offsets.reshape(1, -1)
    o_here, dq_here, there, terms, mine_here = attention(
        where, offsets, queries, cotangent, q_there, do_there, seen, heads_of(kv, core), own_there
    )

    terms = within_ring(terms)
    shifted = ring_shift(theirs_sum(where, terms), -1)
    terms = terms.reshape(RING // 2, 2, TOK, 2 * HEAD)

    def side_by_side(a):
        return jnp.concatenate([a[0, :, :HEAD], a[1, :, :HEAD], a[0, :, HEAD:], a[1, :, HEAD:]], 1)

    after = sum(
        jnp.where(j > chip, terms[j], jnp.zeros_like(terms[j])).astype(F32)
        for j in range(1, RING // 2)
    )
    back = to_sibling(there)
    half = o_here.shape[1]

    def joined(a, b):
        return jnp.where(core == 0, jnp.concatenate([a, b], 1), jnp.concatenate([b, a], 1))

    attended, grad_q = joined(o_here, back[:, :half]), joined(dq_here, back[:, half : 2 * half])
    local = jnp.where(
        core == 0,
        jnp.stack([mine_here, back[:, 2 * half :]]),
        jnp.stack([back[:, 2 * half :], mine_here]),
    )
    ours = side_by_side(after + local.astype(F32))
    ours, attended, grad_q = lax.optimization_barrier((ours, attended, grad_q))
    total = (ours + shifted.astype(F32)).astype(BF16)
    return attended, grad_q, total[:, : 2 * HEAD], total[:, 2 * HEAD :]


def solution(mesh):
    split = P(("blk", "uly"), None)
    return jax.shard_map(
        shards,
        mesh=mesh,
        in_specs=(split, split, split, split, P()),
        out_specs=(split, split, split, split),
        check_vma=False,
    )
```

```python
import functools
import math

import jax
import jax.numpy as jnp
from jax import lax
from jax.experimental import pallas as pl
from jax.experimental.pallas import tpu as pltpu
from jax.sharding import PartitionSpec as P

HEAD = 128
TOK = 128
RING = 8
KEYS = RING * TOK
SPAN = KEYS + TOK
SCALE = 1.0 / math.sqrt(HEAD)
SCALE2 = SCALE * math.log2(math.e)
F32 = jnp.float32
BF16 = jnp.bfloat16


def dot(a, b, ca, cb):
    return lax.dot_general(a, b, (((ca,), (cb,)), ((), ())), preferred_element_type=F32)


def stacked(ref):
    return jnp.concatenate([ref[:, r * HEAD : (r + 1) * HEAD] for r in range(ref.shape[1] // HEAD)], 0)


def attention_kernel(
    where_ref,
    offsets_ref,
    q_here_ref,
    do_here_ref,
    q_there_ref,
    do_there_ref,
    seen_ref,
    own_here_ref,
    own_there_ref,
    o_here_ref,
    dq_here_ref,
    there_ref,
    terms_ref,
    mine_here_ref,
    q_side,
    do_side,
    seen_now,
    own_side,
    k_fill,
    k_zero,
    v_zero,
    o_side,
    dq_side,
    terms_now,
    own_out,
    dk_acc,
    dv_acc,
    sems,
):
    core, chip = where_ref[0], where_ref[1]
    side = pl.program_id(0)
    index = lax.rem(core + side, 2)
    half = o_side.shape[2]
    first_token = where_ref[2] + index * TOK
    offsets = offsets_ref[...]
    start = jnp.max(jnp.where(offsets <= first_token, offsets, 0))
    before = lax.shift_right_logical(first_token - start, 7)

    def slot(m):
        return lax.rem(2 * chip + 1 + m, RING)

    mine = pl.ds(pl.multiple_of(core * half, half), half)
    fetches = [
        [
            pltpu.make_async_copy(q_here_ref.at[:, mine], q_side.at[0], sems.at[0]),
            pltpu.make_async_copy(do_here_ref.at[:, mine], do_side.at[0], sems.at[1]),
            pltpu.make_async_copy(seen_ref, seen_now, sems.at[10]),
            pltpu.make_async_copy(own_here_ref, own_side.at[0], sems.at[11]),
            pltpu.make_async_copy(own_there_ref, own_side.at[1], sems.at[12]),
        ],
        [
            pltpu.make_async_copy(q_there_ref, q_side.at[1], sems.at[2]),
            pltpu.make_async_copy(do_there_ref, do_side.at[1], sems.at[3]),
        ],
    ]

    own_cols = pl.ds(2 * half, 2 * HEAD)
    sends = [
        [
            pltpu.make_async_copy(o_side.at[0], o_here_ref, sems.at[4]),
            pltpu.make_async_copy(dq_side.at[0], dq_here_ref, sems.at[5]),
        ],
        [
            pltpu.make_async_copy(o_side.at[1], there_ref.at[:, pl.ds(0, half)], sems.at[6]),
            pltpu.make_async_copy(dq_side.at[1], there_ref.at[:, pl.ds(half, half)], sems.at[7]),
            pltpu.make_async_copy(own_out, there_ref.at[:, own_cols], sems.at[8]),
        ],
    ]

    @pl.when(side == 0)
    def _():
        for fetch in fetches[0][2:] + fetches[0][:2] + fetches[1]:
            fetch.start()
        dk_acc[...] = jnp.zeros_like(dk_acc)
        dv_acc[...] = jnp.zeros_like(dv_acc)

    @pl.when(side == 0)
    def _():
        for fetch in fetches[0][2:]:
            fetch.wait()

    own_now = own_side.at[side]
    first = jnp.broadcast_to(own_now[0:1, :HEAD], (TOK, HEAD))
    zero = jnp.zeros((TOK, HEAD), BF16)
    for w in range(RING - 1):
        at = slice(w * TOK, (w + 1) * TOK)
        block = seen_now[slot(w + index)]
        if w == RING - 2:
            block = jnp.where(index == 1, own_side[core], block)
        shown = RING - 1 - w <= before
        k_fill[at] = jnp.where(shown, block[:, :HEAD], first)
        k_zero[at] = jnp.where(shown, block[:, :HEAD], zero)
        v_zero[at] = jnp.where(shown, block[:, HEAD:], zero)
    last = slice(KEYS - TOK, KEYS)
    k_fill[last] = own_now[:, :HEAD]
    k_zero[last] = own_now[:, :HEAD]
    v_zero[last] = own_now[:, HEAD:]

    @pl.when(side == 0)
    def _():
        for fetch in fetches[0][:2]:
            fetch.wait()

    @pl.when(side == 1)
    def _():
        for fetch in fetches[1]:
            fetch.wait()

    def attend(tiles):
        width = 2 * tiles * TOK
        heads = half // HEAD
        hidden = 2 * tiles - 1 - before
        row = lax.broadcasted_iota(jnp.int32, (TOK, TOK), 0)
        col = lax.broadcasted_iota(jnp.int32, (TOK, TOK), 1)
        causal = jnp.where(col <= row, 0.0, -1e30).astype(F32)
        k, kz, v = k_fill[KEYS - width :], k_zero[KEYS - width :], v_zero[KEYS - width :]
        group_size = 8
        groups = range(0, heads, group_size)

        def rows_of(ref, g):
            at = ref.at[side]
            return jnp.concatenate([at[:, (g + r) * HEAD : (g + r + 1) * HEAD] for r in range(group_size)], 0)

        qs = [rows_of(q_side, g) for g in groups]
        scores = [dot(q, k, 1, 1) for q in qs]
        dss, ps, norms = [], [], []
        for g, s in zip(groups, scores):
            do = rows_of(do_side, g)
            s = jnp.concatenate(
                [s[:, : width - TOK], s[:, width - TOK :] + jnp.concatenate([causal] * group_size, 0)], 1
            )
            top = jnp.max(s, axis=1, keepdims=True)
            p = jnp.exp2(s * SCALE2 - top * SCALE2)
            p_low = p.astype(BF16)
            wide = p[:, :TOK]
            for w in range(1, 2 * tiles):
                wide = wide + p[:, w * TOK : (w + 1) * TOK]
            total = jnp.sum(wide - hidden.astype(F32) * p[:, :TOK], axis=1, keepdims=True)
            inv = 1.0 / total
            o = (dot(p_low, v, 1, 0) * inv).astype(BF16)
            do_wide = do.astype(F32)
            delta = jnp.sum(do_wide * o.astype(F32), axis=1, keepdims=True) * inv
            do_norm = (do_wide * inv).astype(BF16)
            ds = p_low * (dot(do_norm, v, 1, 1) - delta).astype(BF16)
            dq = (dot(ds, kz, 1, 0) * SCALE).astype(BF16)
            for r in range(group_size):
                at = slice((g + r) * HEAD, (g + r + 1) * HEAD)
                o_side[side, :, at] = o[r * TOK : (r + 1) * TOK]
                dq_side[side, :, at] = dq[r * TOK : (r + 1) * TOK]
            dss.append(ds)
            ps.append(p_low)
            norms.append(do_norm)
        ds, p_low, do_norm, q = [jnp.concatenate(x, 0) for x in (dss, ps, norms, qs)]
        place = lax.broadcasted_iota(jnp.int32, (HEAD, width), 1)
        shown = place >= hidden * TOK
        window = pl.ds(pl.multiple_of(index * TOK + KEYS - width, TOK), width)
        dk_acc[:, window] += jnp.where(shown, dot(q.T, ds, 1, 0), 0.0)
        dv_acc[:, window] += jnp.where(shown, dot(do_norm.T, p_low, 1, 0), 0.0)

    for tiles in range(1, RING // 2 + 1):
        pl.when(lax.shift_right_logical(before, 1) == tiles - 1)(functools.partial(attend, tiles))

    @pl.when(side == 0)
    def _():
        for send in sends[0]:
            send.start()

    @pl.when(side == 1)
    def _():
        for send in sends[1][:2]:
            send.start()

        def part(m):
            return pltpu.make_async_copy(terms_now.at[slot(m)], terms_ref.at[slot(m)], sems.at[13 + m])

        def block(m):
            cols = slice(m * TOK, (m + 1) * TOK)
            return (dk_acc[:, cols] * SCALE).T.astype(BF16), dv_acc[:, cols].T.astype(BF16)

        for m in range(RING - 1):
            terms_now[slot(m), :, :HEAD], terms_now[slot(m), :, HEAD:] = block(m)
            part(m).start()
        terms_now[2 * chip] = jnp.zeros((TOK, 2 * HEAD), BF16)
        part(RING - 1).start()
        even_k, even_v = block(RING - 1)
        odd_k, odd_v = block(RING)
        swap = core == 1
        mine_here_ref[:, :HEAD] = jnp.where(swap, odd_k, even_k)
        mine_here_ref[:, HEAD:] = jnp.where(swap, odd_v, even_v)
        own_out[:, :HEAD] = jnp.where(swap, even_k, odd_k)
        own_out[:, HEAD:] = jnp.where(swap, even_v, odd_v)
        sends[1][2].start()
        for send in sends[0] + sends[1] + [part(m) for m in range(RING)]:
            send.wait()


def attention(where, offsets, queries, cotangent, q_there, do_there, seen, own_here, own_there):
    half = q_there.shape
    rows = half[1] // HEAD * TOK
    own = own_here.shape
    there = (TOK, 2 * half[1] + own[1])
    vmem = pl.BlockSpec(memory_space=pltpu.VMEM)
    anywhere = pl.BlockSpec(memory_space=pl.ANY)
    return pl.pallas_call(
        attention_kernel,
        grid_spec=pltpu.PrefetchScalarGridSpec(
            num_scalar_prefetch=1,
            grid=(2,),
            in_specs=[vmem] + [anywhere] * 7,
            out_specs=[anywhere] * 4 + [vmem],
            scratch_shapes=[
                pltpu.VMEM((2, *half), BF16),
                pltpu.VMEM((2, *half), BF16),
                pltpu.VMEM(seen.shape, BF16),
                pltpu.VMEM((2, *own), BF16),
                pltpu.VMEM((KEYS, HEAD), BF16),
                pltpu.VMEM((KEYS, HEAD), BF16),
                pltpu.VMEM((KEYS, HEAD), BF16),
                pltpu.VMEM((2, *half), BF16),
                pltpu.VMEM((2, *half), BF16),
                pltpu.VMEM(seen.shape, BF16),
                pltpu.VMEM(own, BF16),
                pltpu.VMEM((HEAD, SPAN), F32),
                pltpu.VMEM((HEAD, SPAN), F32),
                pltpu.SemaphoreType.DMA((13 + RING,)),
            ],
        ),
        out_shape=[
            jax.ShapeDtypeStruct(half, BF16),
            jax.ShapeDtypeStruct(half, BF16),
            jax.ShapeDtypeStruct(there, BF16),
            jax.ShapeDtypeStruct(seen.shape, BF16),
            jax.ShapeDtypeStruct(own, BF16),
        ],
        compiler_params=pltpu.CompilerParams(
            vmem_limit_bytes=60 << 20, dimension_semantics=("arbitrary",)
        ),
        cost_estimate=pl.CostEstimate(
            flops=24 * rows * KEYS * HEAD,
            bytes_accessed=16 * rows * HEAD,
            transcendentals=2 * rows * KEYS,
        ),
    )(where, offsets, queries, cotangent, q_there, do_there, seen, own_here, own_there)


def theirs_kernel(where_ref, terms_ref, out_ref):
    chip = where_ref[1]
    for group in range(2):
        total = terms_ref[group].astype(F32)
        for j in range(1, RING // 2):
            total += jnp.where(j > chip, 0.0, terms_ref[2 * j + group].astype(F32))
        k_at, v_at = group * HEAD, (2 + group) * HEAD
        out_ref[:, k_at : k_at + HEAD] = total[:, :HEAD].astype(BF16)
        out_ref[:, v_at : v_at + HEAD] = total[:, HEAD:].astype(BF16)


def theirs_sum(where, terms):
    vmem = pl.BlockSpec(memory_space=pltpu.VMEM)
    return pl.pallas_call(
        theirs_kernel,
        grid_spec=pltpu.PrefetchScalarGridSpec(
            num_scalar_prefetch=1, grid=(1,), in_specs=[vmem], out_specs=vmem
        ),
        out_shape=jax.ShapeDtypeStruct((TOK, 4 * HEAD), BF16),
        compiler_params=pltpu.CompilerParams(vmem_limit_bytes=6 << 20),
        cost_estimate=pl.CostEstimate(flops=40_000_000_000, bytes_accessed=terms.size * 2, transcendentals=0),
    )(where, terms)


def ring_shift(block, rings):
    lanes, regions = lax.axis_size("uly"), lax.axis_size("blk")
    tokens = lanes * regions

    def device(place):
        return (place % lanes) * regions + place // lanes

    route = [
        (device(i), device(i + rings * RING)) for i in range(tokens) if 0 <= i + rings * RING < tokens
    ]
    return lax.ppermute(block, ("uly", "blk"), route)


def within_ring(blocks):
    lanes = lax.axis_size("uly")
    groups = [list(range(r, r + RING)) for r in range(0, lanes, RING)]
    return lax.all_to_all(blocks, "uly", 0, 0, axis_index_groups=groups, tiled=True)


def to_sibling(block):
    lanes = lax.axis_size("uly")
    return lax.ppermute(block, "uly", [(i, i ^ 1) for i in range(lanes)])


def to_sibling(block):
    lanes = lax.axis_size("uly")
    return lax.ppermute(block, "uly", [(i, i ^ 1) for i in range(lanes)])


def shards(queries, keys, values, cotangent, doc_offsets):
    lane = lax.axis_index("uly")
    core, chip = lane & 1, (lane >> 1) & (RING // 2 - 1)
    first = (lax.axis_index("blk") * lax.axis_size("uly") + lane - core) * TOK
    where = jnp.stack([core, chip, first]).astype(jnp.int32)
    slot_chip = (jnp.arange(RING) // 2)[:, None, None]

    def heads_of(block, group):
        width = block.shape[1] // 2
        return lax.dynamic_slice_in_dim(block, group * width, width, 1)

    def by_slot(block):
        return jnp.broadcast_to(
            block.reshape(1, TOK, 2, 2 * HEAD).transpose(0, 2, 1, 3), (RING // 2, 2, TOK, 2 * HEAD)
        ).reshape(RING, TOK, 2 * HEAD)

    kv = jnp.concatenate([keys[:, :HEAD], values[:, :HEAD], keys[:, HEAD:], values[:, HEAD:]], 1)
    behind = ring_shift(kv, 1)
    send = jnp.where(slot_chip > chip, by_slot(kv), by_slot(behind))
    halves = [heads_of(a, 1 - core) for a in (queries, cotangent, kv)]
    where, *halves = lax.optimization_barrier((where, *halves))
    seen = within_ring(send)
    q_there, do_there, own_there = [to_sibling(a) for a in halves]
    offsets = doc_offsets.reshape(1, -1)
    o_here, dq_here, there, terms, mine_here = attention(
        where, offsets, queries, cotangent, q_there, do_there, seen, heads_of(kv, core), own_there
    )

    terms = within_ring(terms)
    shifted = ring_shift(theirs_sum(where, terms), -1)
    terms = terms.reshape(RING // 2, 2, TOK, 2 * HEAD)

    def side_by_side(a):
        return jnp.concatenate([a[0, :, :HEAD], a[1, :, :HEAD], a[0, :, HEAD:], a[1, :, HEAD:]], 1)

    after = sum(
        jnp.where(j > chip, terms[j], jnp.zeros_like(terms[j])).astype(F32)
        for j in range(1, RING // 2)
    )
    back = to_sibling(there)
    half = o_here.shape[1]

    def joined(a, b):
        return jnp.where(core == 0, jnp.concatenate([a, b], 1), jnp.concatenate([b, a], 1))

    attended, grad_q = joined(o_here, back[:, :half]), joined(dq_here, back[:, half : 2 * half])
    local = jnp.where(
        core == 0,
        jnp.stack([mine_here, back[:, 2 * half :]]),
        jnp.stack([back[:, 2 * half :], mine_here]),
    )
    ours = side_by_side(after + local.astype(F32))
    ours, attended, grad_q = lax.optimization_barrier((ours, attended, grad_q))
    total = (ours + shifted.astype(F32)).astype(BF16)
    return attended, grad_q, total[:, : 2 * HEAD], total[:, 2 * HEAD :]


def solution(mesh):
    split = P(("blk", "uly"), None)
    return jax.shard_map(
        shards,
        mesh=mesh,
        in_specs=(split, split, split, split, P()),
        out_specs=(split, split, split, split),
        check_vma=False,
    )
```

```python
import functools
import math

import jax
import jax.numpy as jnp
from jax import lax
from jax.experimental import pallas as pl
from jax.experimental.pallas import tpu as pltpu
from jax.sharding import PartitionSpec as P

HEAD = 128
TOK = 128
RING = 8
KEYS = RING * TOK
SPAN = KEYS + TOK
SCALE = 1.0 / math.sqrt(HEAD)
SCALE2 = SCALE * math.log2(math.e)
F32 = jnp.float32
BF16 = jnp.bfloat16
STEP_ROWS = 2048


def dot(a, b, ca, cb):
    return lax.dot_general(a, b, (((ca,), (cb,)), ((), ())), preferred_element_type=F32)


def stacked(ref):
    return jnp.concatenate([ref[:, r * HEAD : (r + 1) * HEAD] for r in range(ref.shape[1] // HEAD)], 0)


def attention_kernel(
    where_ref,
    offsets_ref,
    q_here_ref,
    do_here_ref,
    q_there_ref,
    do_there_ref,
    seen_ref,
    own_here_ref,
    own_there_ref,
    o_here_ref,
    there_ref,
    terms_ref,
    ds_ref,
    keys_ref,
    mine_here_ref,
    q_side,
    do_side,
    seen_now,
    own_side,
    k_fill,
    k_zero,
    v_zero,
    o_side,
    ds_side,
    terms_now,
    own_out,
    dk_acc,
    dv_acc,
    sems,
):
    core, chip = where_ref[0], where_ref[1]
    side = pl.program_id(0)
    index = lax.rem(core + side, 2)
    half = o_side.shape[2]
    first_token = where_ref[2] + index * TOK
    offsets = offsets_ref[...]
    start = jnp.max(jnp.where(offsets <= first_token, offsets, 0))
    before = lax.shift_right_logical(first_token - start, 7)

    def slot(m):
        return lax.rem(2 * chip + 1 + m, RING)

    mine = pl.ds(pl.multiple_of(core * half, half), half)
    fetches = [
        [
            pltpu.make_async_copy(q_here_ref.at[:, mine], q_side.at[0], sems.at[0]),
            pltpu.make_async_copy(do_here_ref.at[:, mine], do_side.at[0], sems.at[1]),
            pltpu.make_async_copy(seen_ref, seen_now, sems.at[10]),
            pltpu.make_async_copy(own_here_ref, own_side.at[0], sems.at[11]),
            pltpu.make_async_copy(own_there_ref, own_side.at[1], sems.at[12]),
        ],
        [
            pltpu.make_async_copy(q_there_ref, q_side.at[1], sems.at[2]),
            pltpu.make_async_copy(do_there_ref, do_side.at[1], sems.at[3]),
        ],
    ]

    own_cols = pl.ds(half, 2 * HEAD)
    rows = half // HEAD * TOK
    sends = [
        [
            pltpu.make_async_copy(o_side.at[0], o_here_ref, sems.at[4]),
        ],
        [
            pltpu.make_async_copy(o_side.at[1], there_ref.at[:, pl.ds(0, half)], sems.at[6]),
            pltpu.make_async_copy(own_out, there_ref.at[:, own_cols], sems.at[8]),
        ],
    ]

    def keep(side, what):
        if what == 0:
            return pltpu.make_async_copy(ds_side.at[side], ds_ref.at[pl.ds(side * rows, rows)], sems.at[5 + 2 * side])
        return pltpu.make_async_copy(k_zero.at[side], keys_ref.at[side], sems.at[9 + 12 * side])

    @pl.when(side == 0)
    def _():
        for fetch in fetches[0][2:] + fetches[0][:2] + fetches[1]:
            fetch.start()
        dk_acc[...] = jnp.zeros_like(dk_acc)
        dv_acc[...] = jnp.zeros_like(dv_acc)

    @pl.when(side == 0)
    def _():
        for fetch in fetches[0][2:]:
            fetch.wait()

    own_now = own_side.at[side]
    first = jnp.broadcast_to(own_now[0:1, :HEAD], (TOK, HEAD))
    zero = jnp.zeros((TOK, HEAD), BF16)
    for w in range(RING - 1):
        at = slice(w * TOK, (w + 1) * TOK)
        block = seen_now[slot(w + index)]
        if w == RING - 2:
            block = jnp.where(index == 1, own_side[core], block)
        shown = RING - 1 - w <= before
        k_fill[at] = jnp.where(shown, block[:, :HEAD], first)
        k_zero[side, at] = jnp.where(shown, block[:, :HEAD], zero)
        v_zero[at] = jnp.where(shown, block[:, HEAD:], zero)
    last = slice(KEYS - TOK, KEYS)
    k_fill[last] = own_now[:, :HEAD]
    k_zero[side, last] = own_now[:, :HEAD]
    v_zero[last] = own_now[:, HEAD:]

    @pl.when(side == 0)
    def _():
        for fetch in fetches[0][:2]:
            fetch.wait()

    @pl.when(side == 1)
    def _():
        for fetch in fetches[1]:
            fetch.wait()

    def start_kept(n):
        @pl.when(side == n)
        def _():
            keep(n, 0).start()
            keep(n, 1).start()

    def attend(tiles):
        width = 2 * tiles * TOK
        heads = half // HEAD
        hidden = 2 * tiles - 1 - before
        row = lax.broadcasted_iota(jnp.int32, (TOK, TOK), 0)
        col = lax.broadcasted_iota(jnp.int32, (TOK, TOK), 1)
        causal = jnp.where(col <= row, 0.0, -1e30).astype(F32)
        k, v = k_fill[KEYS - width :], v_zero[KEYS - width :]
        group_size = 8
        groups = range(0, heads, group_size)

        def rows_of(ref, g):
            at = ref.at[side]
            return jnp.concatenate([at[:, (g + r) * HEAD : (g + r + 1) * HEAD] for r in range(group_size)], 0)

        qs = [rows_of(q_side, g) for g in groups]
        scores = [dot(q, k, 1, 1) for q in qs]
        dss, ps, norms = [], [], []
        for g, s in zip(groups, scores):
            do = rows_of(do_side, g)
            s = jnp.concatenate(
                [s[:, : width - TOK], s[:, width - TOK :] + jnp.concatenate([causal] * group_size, 0)], 1
            )
            top = jnp.max(s, axis=1, keepdims=True)
            p = jnp.exp2(s * SCALE2 - top * SCALE2)
            p_low = p.astype(BF16)
            wide = p[:, :TOK]
            for w in range(1, 2 * tiles):
                wide = wide + p[:, w * TOK : (w + 1) * TOK]
            total = jnp.sum(wide - hidden.astype(F32) * p[:, :TOK], axis=1, keepdims=True)
            inv = 1.0 / total
            o = (dot(p_low, v, 1, 0) * inv).astype(BF16)
            do_wide = do.astype(F32)
            delta = jnp.sum(do_wide * o.astype(F32), axis=1, keepdims=True) * inv
            do_norm = (do_wide * inv).astype(BF16)
            ds = p_low * (dot(do_norm, v, 1, 1) - delta).astype(BF16)
            for r in range(group_size):
                at = slice((g + r) * HEAD, (g + r + 1) * HEAD)
                o_side[side, :, at] = o[r * TOK : (r + 1) * TOK]
            at = pl.ds(g * TOK, group_size * TOK)
            ds_side[side, at, KEYS - width :] = ds
            if width < KEYS:
                ds_side[side, at, : KEYS - width] = jnp.zeros((group_size * TOK, KEYS - width), BF16)
            dss.append(ds)
            ps.append(p_low)
            norms.append(do_norm)
        for n in range(2):
            start_kept(n)
        ds, p_low, do_norm, q = [jnp.concatenate(x, 0) for x in (dss, ps, norms, qs)]
        place = lax.broadcasted_iota(jnp.int32, (HEAD, width), 1)
        shown = place >= hidden * TOK
        window = pl.ds(pl.multiple_of(index * TOK + KEYS - width, TOK), width)
        dk_acc[:, window] += jnp.where(shown, dot(q.T, ds, 1, 0), 0.0)
        dv_acc[:, window] += jnp.where(shown, dot(do_norm.T, p_low, 1, 0), 0.0)

    for tiles in range(1, RING // 2 + 1):
        pl.when(lax.shift_right_logical(before, 1) == tiles - 1)(functools.partial(attend, tiles))

    @pl.when(side == 0)
    def _():
        for send in sends[0]:
            send.start()

    @pl.when(side == 1)
    def _():
        sends[1][0].start()

        def part(m):
            return pltpu.make_async_copy(terms_now.at[slot(m)], terms_ref.at[slot(m)], sems.at[13 + m])

        def block(m):
            cols = slice(m * TOK, (m + 1) * TOK)
            return (dk_acc[:, cols] * SCALE).T.astype(BF16), dv_acc[:, cols].T.astype(BF16)

        for m in range(RING - 1):
            terms_now[slot(m), :, :HEAD], terms_now[slot(m), :, HEAD:] = block(m)
            part(m).start()
        terms_now[2 * chip] = jnp.zeros((TOK, 2 * HEAD), BF16)
        part(RING - 1).start()
        even_k, even_v = block(RING - 1)
        odd_k, odd_v = block(RING)
        swap = core == 1
        mine_here_ref[:, :HEAD] = jnp.where(swap, odd_k, even_k)
        mine_here_ref[:, HEAD:] = jnp.where(swap, odd_v, even_v)
        own_out[:, :HEAD] = jnp.where(swap, even_k, odd_k)
        own_out[:, HEAD:] = jnp.where(swap, even_v, odd_v)
        sends[1][1].start()
        kept = [keep(n, what) for n in range(2) for what in range(2)]
        for send in sends[0] + sends[1] + kept + [part(m) for m in range(RING)]:
            send.wait()


def attention(where, offsets, queries, cotangent, q_there, do_there, seen, own_here, own_there):
    half = q_there.shape
    rows = half[1] // HEAD * TOK
    own = own_here.shape
    there = (TOK, half[1] + own[1])
    vmem = pl.BlockSpec(memory_space=pltpu.VMEM)
    anywhere = pl.BlockSpec(memory_space=pl.ANY)
    return pl.pallas_call(
        attention_kernel,
        grid_spec=pltpu.PrefetchScalarGridSpec(
            num_scalar_prefetch=1,
            grid=(2,),
            in_specs=[vmem] + [anywhere] * 7,
            out_specs=[anywhere] * 5 + [vmem],
            scratch_shapes=[
                pltpu.VMEM((2, *half), BF16),
                pltpu.VMEM((2, *half), BF16),
                pltpu.VMEM(seen.shape, BF16),
                pltpu.VMEM((2, *own), BF16),
                pltpu.VMEM((KEYS, HEAD), BF16),
                pltpu.VMEM((2, KEYS, HEAD), BF16),
                pltpu.VMEM((KEYS, HEAD), BF16),
                pltpu.VMEM((2, *half), BF16),
                pltpu.VMEM((2, rows, KEYS), BF16),
                pltpu.VMEM(seen.shape, BF16),
                pltpu.VMEM(own, BF16),
                pltpu.VMEM((HEAD, SPAN), F32),
                pltpu.VMEM((HEAD, SPAN), F32),
                pltpu.SemaphoreType.DMA((14 + RING,)),
            ],
        ),
        out_shape=[
            jax.ShapeDtypeStruct(half, BF16),
            jax.ShapeDtypeStruct(there, BF16),
            jax.ShapeDtypeStruct(seen.shape, BF16),
            jax.ShapeDtypeStruct((2 * rows, KEYS), BF16),
            jax.ShapeDtypeStruct((2, KEYS, HEAD), BF16),
            jax.ShapeDtypeStruct(own, BF16),
        ],
        compiler_params=pltpu.CompilerParams(
            vmem_limit_bytes=60 << 20, dimension_semantics=("arbitrary",)
        ),
        cost_estimate=pl.CostEstimate(
            flops=24 * rows * KEYS * HEAD,
            bytes_accessed=16 * rows * HEAD,
            transcendentals=2 * rows * KEYS,
        ),
    )(where, offsets, queries, cotangent, q_there, do_there, seen, own_here, own_there)


def queries_kernel(ds_ref, keys_ref, dq_here_ref, dq_there_ref):
    dq = (dot(ds_ref[...], keys_ref[0], 1, 0) * SCALE).astype(BF16)
    steps = pl.num_programs(0) // 2

    def put(ref):
        for r in range(dq.shape[0] // TOK):
            ref[:, r * HEAD : (r + 1) * HEAD] = dq[r * TOK : (r + 1) * TOK]

    @pl.when(pl.program_id(0) < steps)
    def _():
        put(dq_here_ref)

    @pl.when(pl.program_id(0) >= steps)
    def _():
        put(dq_there_ref)


def queries_gradient(ds, keys, half):
    steps = ds.shape[0] // 2 // STEP_ROWS
    block = (TOK, half[1] // steps)
    return pl.pallas_call(
        queries_kernel,
        grid=(2 * steps,),
        in_specs=[
            pl.BlockSpec((STEP_ROWS, KEYS), lambda i: (i, 0)),
            pl.BlockSpec((1, KEYS, HEAD), lambda i: (i // steps, 0, 0)),
        ],
        out_specs=[
            pl.BlockSpec(block, lambda i: (0, jnp.minimum(i, steps - 1))),
            pl.BlockSpec(block, lambda i: (0, jnp.maximum(i - steps, 0))),
        ],
        out_shape=[jax.ShapeDtypeStruct(half, BF16)] * 2,
        compiler_params=pltpu.CompilerParams(
            vmem_limit_bytes=40 << 20, dimension_semantics=("arbitrary",)
        ),
        cost_estimate=pl.CostEstimate(
            flops=2 * ds.size * HEAD, bytes_accessed=2 * ds.size, transcendentals=0
        ),
    )(ds, keys)


def theirs_kernel(where_ref, terms_ref, out_ref):
    chip = where_ref[1]
    for group in range(2):
        total = terms_ref[group].astype(F32)
        for j in range(1, RING // 2):
            total += jnp.where(j > chip, 0.0, terms_ref[2 * j + group].astype(F32))
        k_at, v_at = group * HEAD, (2 + group) * HEAD
        out_ref[:, k_at : k_at + HEAD] = total[:, :HEAD].astype(BF16)
        out_ref[:, v_at : v_at + HEAD] = total[:, HEAD:].astype(BF16)


def theirs_sum(where, terms):
    vmem = pl.BlockSpec(memory_space=pltpu.VMEM)
    return pl.pallas_call(
        theirs_kernel,
        grid_spec=pltpu.PrefetchScalarGridSpec(
            num_scalar_prefetch=1, grid=(1,), in_specs=[vmem], out_specs=vmem
        ),
        out_shape=jax.ShapeDtypeStruct((TOK, 4 * HEAD), BF16),
        compiler_params=pltpu.CompilerParams(vmem_limit_bytes=6 << 20),
        cost_estimate=pl.CostEstimate(flops=40_000_000_000, bytes_accessed=terms.size * 2, transcendentals=0),
    )(where, terms)


def ring_shift(block, rings):
    lanes, regions = lax.axis_size("uly"), lax.axis_size("blk")
    tokens = lanes * regions

    def device(place):
        return (place % lanes) * regions + place // lanes

    route = [
        (device(i), device(i + rings * RING)) for i in range(tokens) if 0 <= i + rings * RING < tokens
    ]
    return lax.ppermute(block, ("uly", "blk"), route)


def within_ring(blocks):
    lanes = lax.axis_size("uly")
    groups = [list(range(r, r + RING)) for r in range(0, lanes, RING)]
    return lax.all_to_all(blocks, "uly", 0, 0, axis_index_groups=groups, tiled=True)


def to_sibling(block):
    lanes = lax.axis_size("uly")
    return lax.ppermute(block, "uly", [(i, i ^ 1) for i in range(lanes)])


def to_sibling(block):
    lanes = lax.axis_size("uly")
    return lax.ppermute(block, "uly", [(i, i ^ 1) for i in range(lanes)])


def shards(queries, keys, values, cotangent, doc_offsets):
    lane = lax.axis_index("uly")
    core, chip = lane & 1, (lane >> 1) & (RING // 2 - 1)
    first = (lax.axis_index("blk") * lax.axis_size("uly") + lane - core) * TOK
    where = jnp.stack([core, chip, first]).astype(jnp.int32)
    slot_chip = (jnp.arange(RING) // 2)[:, None, None]

    def heads_of(block, group):
        width = block.shape[1] // 2
        return lax.dynamic_slice_in_dim(block, group * width, width, 1)

    def by_slot(block):
        return jnp.broadcast_to(
            block.reshape(1, TOK, 2, 2 * HEAD).transpose(0, 2, 1, 3), (RING // 2, 2, TOK, 2 * HEAD)
        ).reshape(RING, TOK, 2 * HEAD)

    kv = jnp.concatenate([keys[:, :HEAD], values[:, :HEAD], keys[:, HEAD:], values[:, HEAD:]], 1)
    behind = ring_shift(kv, 1)
    send = jnp.where(slot_chip > chip, by_slot(kv), by_slot(behind))
    halves = [heads_of(a, 1 - core) for a in (queries, cotangent, kv)]
    where, *halves = lax.optimization_barrier((where, *halves))
    seen = within_ring(send)
    q_there, do_there, own_there = [to_sibling(a) for a in halves]
    offsets = doc_offsets.reshape(1, -1)
    o_here, there, terms, ds, kept_keys, mine_here = attention(
        where, offsets, queries, cotangent, q_there, do_there, seen, heads_of(kv, core), own_there
    )

    terms = within_ring(terms)
    shifted = ring_shift(theirs_sum(where, terms), -1)
    terms = terms.reshape(RING // 2, 2, TOK, 2 * HEAD)

    def side_by_side(a):
        return jnp.concatenate([a[0, :, :HEAD], a[1, :, :HEAD], a[0, :, HEAD:], a[1, :, HEAD:]], 1)

    after = sum(
        jnp.where(j > chip, terms[j], jnp.zeros_like(terms[j])).astype(F32)
        for j in range(1, RING // 2)
    )
    dq_here, dq_there = queries_gradient(ds, kept_keys, o_here.shape)
    back, dq_back = to_sibling(there), to_sibling(dq_there)
    half = o_here.shape[1]

    def joined(a, b):
        return jnp.where(core == 0, jnp.concatenate([a, b], 1), jnp.concatenate([b, a], 1))

    attended, grad_q = joined(o_here, back[:, :half]), joined(dq_here, dq_back)
    local = jnp.where(
        core == 0,
        jnp.stack([mine_here, back[:, half:]]),
        jnp.stack([back[:, half:], mine_here]),
    )
    ours = side_by_side(after + local.astype(F32))
    ours, attended, grad_q = lax.optimization_barrier((ours, attended, grad_q))
    total = (ours + shifted.astype(F32)).astype(BF16)
    return attended, grad_q, total[:, : 2 * HEAD], total[:, 2 * HEAD :]


def solution(mesh):
    split = P(("blk", "uly"), None)
    return jax.shard_map(
        shards,
        mesh=mesh,
        in_specs=(split, split, split, split, P()),
        out_specs=(split, split, split, split),
        check_vma=False,
    )
```

```python
import functools
import math

import jax
import jax.numpy as jnp
from jax import lax
from jax.experimental import pallas as pl
from jax.experimental.pallas import tpu as pltpu
from jax.sharding import PartitionSpec as P

HEAD = 128
TOK = 128
RING = 8
KEYS = RING * TOK
SPAN = KEYS + TOK
SCALE = 1.0 / math.sqrt(HEAD)
SCALE2 = SCALE * math.log2(math.e)
F32 = jnp.float32
BF16 = jnp.bfloat16


def dot(a, b, ca, cb):
    return lax.dot_general(a, b, (((ca,), (cb,)), ((), ())), preferred_element_type=F32)


def stacked(ref):
    return jnp.concatenate([ref[:, r * HEAD : (r + 1) * HEAD] for r in range(ref.shape[1] // HEAD)], 0)


def attention_kernel(
    where_ref,
    offsets_ref,
    q_here_ref,
    do_here_ref,
    q_there_ref,
    do_there_ref,
    seen_ref,
    own_here_ref,
    own_there_ref,
    o_here_ref,
    dq_here_ref,
    there_ref,
    terms_ref,
    mine_here_ref,
    q_side,
    do_side,
    seen_now,
    own_side,
    k_fill,
    k_zero,
    v_zero,
    o_side,
    dq_side,
    terms_now,
    own_out,
    dk_acc,
    dv_acc,
    sems,
):
    core, chip = where_ref[0], where_ref[1]
    side = pl.program_id(0)
    index = lax.rem(core + side, 2)
    half = o_side.shape[2]
    first_token = where_ref[2] + index * TOK
    offsets = offsets_ref[...]
    start = jnp.max(jnp.where(offsets <= first_token, offsets, 0))
    before = lax.shift_right_logical(first_token - start, 7)

    def slot(m):
        return lax.rem(2 * chip + 1 + m, RING)

    mine = pl.ds(pl.multiple_of(core * half, half), half)
    fetches = [
        [
            pltpu.make_async_copy(q_here_ref.at[:, mine], q_side.at[0], sems.at[0]),
            pltpu.make_async_copy(do_here_ref.at[:, mine], do_side.at[0], sems.at[1]),
            pltpu.make_async_copy(seen_ref, seen_now, sems.at[10]),
            pltpu.make_async_copy(own_here_ref, own_side.at[0], sems.at[11]),
            pltpu.make_async_copy(own_there_ref, own_side.at[1], sems.at[12]),
        ],
        [
            pltpu.make_async_copy(q_there_ref, q_side.at[1], sems.at[2]),
            pltpu.make_async_copy(do_there_ref, do_side.at[1], sems.at[3]),
        ],
    ]

    own_cols = pl.ds(2 * half, 2 * HEAD)
    sends = [
        [
            pltpu.make_async_copy(o_side.at[0], o_here_ref, sems.at[4]),
            pltpu.make_async_copy(dq_side.at[0], dq_here_ref, sems.at[5]),
        ],
        [
            pltpu.make_async_copy(o_side.at[1], there_ref.at[:, pl.ds(0, half)], sems.at[6]),
            pltpu.make_async_copy(dq_side.at[1], there_ref.at[:, pl.ds(half, half)], sems.at[7]),
            pltpu.make_async_copy(own_out, there_ref.at[:, own_cols], sems.at[8]),
        ],
    ]

    @pl.when(side == 0)
    def _():
        for fetch in fetches[0][2:] + fetches[0][:2] + fetches[1]:
            fetch.start()
        dk_acc[...] = jnp.zeros_like(dk_acc)
        dv_acc[...] = jnp.zeros_like(dv_acc)

    @pl.when(side == 0)
    def _():
        for fetch in fetches[0][2:]:
            fetch.wait()

    own_now = own_side.at[side]
    first = jnp.broadcast_to(own_now[0:1, :HEAD], (TOK, HEAD))
    zero = jnp.zeros((TOK, HEAD), BF16)
    for w in range(RING - 1):
        at = slice(w * TOK, (w + 1) * TOK)
        block = seen_now[slot(w + index)]
        if w == RING - 2:
            block = jnp.where(index == 1, own_side[core], block)
        shown = RING - 1 - w <= before
        k_fill[at] = jnp.where(shown, block[:, :HEAD], first)
        k_zero[at] = jnp.where(shown, block[:, :HEAD], zero)
        v_zero[at] = jnp.where(shown, block[:, HEAD:], zero)
    last = slice(KEYS - TOK, KEYS)
    k_fill[last] = own_now[:, :HEAD]
    k_zero[last] = own_now[:, :HEAD]
    v_zero[last] = own_now[:, HEAD:]

    @pl.when(side == 0)
    def _():
        for fetch in fetches[0][:2]:
            fetch.wait()

    @pl.when(side == 1)
    def _():
        for fetch in fetches[1]:
            fetch.wait()

    def start_sends(n):
        @pl.when(side == n)
        def _():
            for send in sends[n][:2]:
                send.start()

    def attend(tiles):
        width = 2 * tiles * TOK
        heads = half // HEAD
        hidden = 2 * tiles - 1 - before
        row = lax.broadcasted_iota(jnp.int32, (TOK, TOK), 0)
        col = lax.broadcasted_iota(jnp.int32, (TOK, TOK), 1)
        causal = jnp.where(col <= row, 0.0, -1e30).astype(F32)
        k, kz, v = k_fill[KEYS - width :], k_zero[KEYS - width :], v_zero[KEYS - width :]
        group_size = 8
        groups = range(0, heads, group_size)

        def rows_of(ref, g):
            at = ref.at[side]
            return jnp.concatenate([at[:, (g + r) * HEAD : (g + r + 1) * HEAD] for r in range(group_size)], 0)

        qs = [rows_of(q_side, g) for g in groups]
        scores = [dot(q, k, 1, 1) for q in qs]
        dss, ps, norms = [], [], []
        for g, s in zip(groups, scores):
            do = rows_of(do_side, g)
            s = jnp.concatenate(
                [s[:, : width - TOK], s[:, width - TOK :] + jnp.concatenate([causal] * group_size, 0)], 1
            )
            top = jnp.max(s, axis=1, keepdims=True)
            p = jnp.exp2(s * SCALE2 - top * SCALE2)
            p_low = p.astype(BF16)
            wide = p[:, :TOK]
            for w in range(1, 2 * tiles):
                wide = wide + p[:, w * TOK : (w + 1) * TOK]
            total = jnp.sum(wide - hidden.astype(F32) * p[:, :TOK], axis=1, keepdims=True)
            inv = 1.0 / total
            o = (dot(p_low, v, 1, 0) * inv).astype(BF16)
            do_wide = do.astype(F32)
            delta = jnp.sum(do_wide * o.astype(F32), axis=1, keepdims=True) * inv
            do_norm = (do_wide * inv).astype(BF16)
            ds = p_low * (dot(do_norm, v, 1, 1) - delta).astype(BF16)
            dq = (dot(ds, kz, 1, 0) * SCALE).astype(BF16)
            for r in range(group_size):
                at = slice((g + r) * HEAD, (g + r + 1) * HEAD)
                o_side[side, :, at] = o[r * TOK : (r + 1) * TOK]
                dq_side[side, :, at] = dq[r * TOK : (r + 1) * TOK]
            dss.append(ds)
            ps.append(p_low)
            norms.append(do_norm)
        for n in range(2):
            start_sends(n)
        ds, p_low, do_norm, q = [jnp.concatenate(x, 0) for x in (dss, ps, norms, qs)]
        place = lax.broadcasted_iota(jnp.int32, (HEAD, width), 1)
        shown = place >= hidden * TOK
        window = pl.ds(pl.multiple_of(index * TOK + KEYS - width, TOK), width)
        dk_acc[:, window] += jnp.where(shown, dot(q.T, ds, 1, 0), 0.0)
        dv_acc[:, window] += jnp.where(shown, dot(do_norm.T, p_low, 1, 0), 0.0)

    for tiles in range(1, RING // 2 + 1):
        pl.when(lax.shift_right_logical(before, 1) == tiles - 1)(functools.partial(attend, tiles))

    @pl.when(side == 1)
    def _():
        def part(m):
            return pltpu.make_async_copy(terms_now.at[slot(m)], terms_ref.at[slot(m)], sems.at[13 + m])

        def block(m):
            cols = slice(m * TOK, (m + 1) * TOK)
            return (dk_acc[:, cols] * SCALE).T.astype(BF16), dv_acc[:, cols].T.astype(BF16)

        for m in range(RING - 1):
            terms_now[slot(m), :, :HEAD], terms_now[slot(m), :, HEAD:] = block(m)
            part(m).start()
        terms_now[2 * chip] = jnp.zeros((TOK, 2 * HEAD), BF16)
        part(RING - 1).start()
        even_k, even_v = block(RING - 1)
        odd_k, odd_v = block(RING)
        swap = core == 1
        mine_here_ref[:, :HEAD] = jnp.where(swap, odd_k, even_k)
        mine_here_ref[:, HEAD:] = jnp.where(swap, odd_v, even_v)
        own_out[:, :HEAD] = jnp.where(swap, even_k, odd_k)
        own_out[:, HEAD:] = jnp.where(swap, even_v, odd_v)
        sends[1][2].start()
        for send in sends[0] + sends[1] + [part(m) for m in range(RING)]:
            send.wait()


def attention(where, offsets, queries, cotangent, q_there, do_there, seen, own_here, own_there):
    half = q_there.shape
    rows = half[1] // HEAD * TOK
    own = own_here.shape
    there = (TOK, 2 * half[1] + own[1])
    vmem = pl.BlockSpec(memory_space=pltpu.VMEM)
    anywhere = pl.BlockSpec(memory_space=pl.ANY)
    return pl.pallas_call(
        attention_kernel,
        grid_spec=pltpu.PrefetchScalarGridSpec(
            num_scalar_prefetch=1,
            grid=(2,),
            in_specs=[vmem] + [anywhere] * 7,
            out_specs=[anywhere] * 4 + [vmem],
            scratch_shapes=[
                pltpu.VMEM((2, *half), BF16),
                pltpu.VMEM((2, *half), BF16),
                pltpu.VMEM(seen.shape, BF16),
                pltpu.VMEM((2, *own), BF16),
                pltpu.VMEM((KEYS, HEAD), BF16),
                pltpu.VMEM((KEYS, HEAD), BF16),
                pltpu.VMEM((KEYS, HEAD), BF16),
                pltpu.VMEM((2, *half), BF16),
                pltpu.VMEM((2, *half), BF16),
                pltpu.VMEM(seen.shape, BF16),
                pltpu.VMEM(own, BF16),
                pltpu.VMEM((HEAD, SPAN), F32),
                pltpu.VMEM((HEAD, SPAN), F32),
                pltpu.SemaphoreType.DMA((13 + RING,)),
            ],
        ),
        out_shape=[
            jax.ShapeDtypeStruct(half, BF16),
            jax.ShapeDtypeStruct(half, BF16),
            jax.ShapeDtypeStruct(there, BF16),
            jax.ShapeDtypeStruct(seen.shape, BF16),
            jax.ShapeDtypeStruct(own, BF16),
        ],
        compiler_params=pltpu.CompilerParams(
            vmem_limit_bytes=62 << 20, dimension_semantics=("arbitrary",)
        ),
        cost_estimate=pl.CostEstimate(
            flops=24 * rows * KEYS * HEAD,
            bytes_accessed=16 * rows * HEAD,
            transcendentals=2 * rows * KEYS,
        ),
    )(where, offsets, queries, cotangent, q_there, do_there, seen, own_here, own_there)


def theirs_kernel(where_ref, terms_ref, out_ref):
    chip = where_ref[1]
    for group in range(2):
        total = terms_ref[group].astype(F32)
        for j in range(1, RING // 2):
            total += jnp.where(j > chip, 0.0, terms_ref[2 * j + group].astype(F32))
        k_at, v_at = group * HEAD, (2 + group) * HEAD
        out_ref[:, k_at : k_at + HEAD] = total[:, :HEAD].astype(BF16)
        out_ref[:, v_at : v_at + HEAD] = total[:, HEAD:].astype(BF16)


def theirs_sum(where, terms):
    vmem = pl.BlockSpec(memory_space=pltpu.VMEM)
    return pl.pallas_call(
        theirs_kernel,
        grid_spec=pltpu.PrefetchScalarGridSpec(
            num_scalar_prefetch=1, grid=(1,), in_specs=[vmem], out_specs=vmem
        ),
        out_shape=jax.ShapeDtypeStruct((TOK, 4 * HEAD), BF16),
        compiler_params=pltpu.CompilerParams(vmem_limit_bytes=6 << 20),
        cost_estimate=pl.CostEstimate(flops=40_000_000_000, bytes_accessed=terms.size * 2, transcendentals=0),
    )(where, terms)


def ring_shift(block, rings):
    lanes, regions = lax.axis_size("uly"), lax.axis_size("blk")
    tokens = lanes * regions

    def device(place):
        return (place % lanes) * regions + place // lanes

    route = [
        (device(i), device(i + rings * RING)) for i in range(tokens) if 0 <= i + rings * RING < tokens
    ]
    return lax.ppermute(block, ("uly", "blk"), route)


def within_ring(blocks):
    lanes = lax.axis_size("uly")
    groups = [list(range(r, r + RING)) for r in range(0, lanes, RING)]
    return lax.all_to_all(blocks, "uly", 0, 0, axis_index_groups=groups, tiled=True)


def to_sibling(block):
    lanes = lax.axis_size("uly")
    return lax.ppermute(block, "uly", [(i, i ^ 1) for i in range(lanes)])


def to_sibling(block):
    lanes = lax.axis_size("uly")
    return lax.ppermute(block, "uly", [(i, i ^ 1) for i in range(lanes)])


def shards(queries, keys, values, cotangent, doc_offsets):
    lane = lax.axis_index("uly")
    core, chip = lane & 1, (lane >> 1) & (RING // 2 - 1)
    first = (lax.axis_index("blk") * lax.axis_size("uly") + lane - core) * TOK
    where = jnp.stack([core, chip, first]).astype(jnp.int32)
    slot_chip = (jnp.arange(RING) // 2)[:, None, None]

    def heads_of(block, group):
        width = block.shape[1] // 2
        return lax.dynamic_slice_in_dim(block, group * width, width, 1)

    def by_slot(block):
        return jnp.broadcast_to(
            block.reshape(1, TOK, 2, 2 * HEAD).transpose(0, 2, 1, 3), (RING // 2, 2, TOK, 2 * HEAD)
        ).reshape(RING, TOK, 2 * HEAD)

    kv = jnp.concatenate([keys[:, :HEAD], values[:, :HEAD], keys[:, HEAD:], values[:, HEAD:]], 1)
    behind = ring_shift(kv, 1)
    send = jnp.where(slot_chip > chip, by_slot(kv), by_slot(behind))
    halves = [heads_of(a, 1 - core) for a in (queries, cotangent, kv)]
    where, *halves = lax.optimization_barrier((where, *halves))
    seen = within_ring(send)
    q_there, do_there, own_there = [to_sibling(a) for a in halves]
    offsets = doc_offsets.reshape(1, -1)
    o_here, dq_here, there, terms, mine_here = attention(
        where, offsets, queries, cotangent, q_there, do_there, seen, heads_of(kv, core), own_there
    )

    terms = within_ring(terms)
    shifted = ring_shift(theirs_sum(where, terms), -1)
    terms = terms.reshape(RING // 2, 2, TOK, 2 * HEAD)

    def side_by_side(a):
        return jnp.concatenate([a[0, :, :HEAD], a[1, :, :HEAD], a[0, :, HEAD:], a[1, :, HEAD:]], 1)

    after = sum(
        jnp.where(j > chip, terms[j], jnp.zeros_like(terms[j])).astype(F32)
        for j in range(1, RING // 2)
    )
    back = to_sibling(there)
    half = o_here.shape[1]

    def joined(a, b):
        return jnp.where(core == 0, jnp.concatenate([a, b], 1), jnp.concatenate([b, a], 1))

    attended, grad_q = joined(o_here, back[:, :half]), joined(dq_here, back[:, half : 2 * half])
    local = jnp.where(
        core == 0,
        jnp.stack([mine_here, back[:, 2 * half :]]),
        jnp.stack([back[:, 2 * half :], mine_here]),
    )
    ours = side_by_side(after + local.astype(F32))
    ours, attended, grad_q = lax.optimization_barrier((ours, attended, grad_q))
    total = (ours + shifted.astype(F32)).astype(BF16)
    return attended, grad_q, total[:, : 2 * HEAD], total[:, 2 * HEAD :]


def solution(mesh):
    split = P(("blk", "uly"), None)
    return jax.shard_map(
        shards,
        mesh=mesh,
        in_specs=(split, split, split, split, P()),
        out_specs=(split, split, split, split),
        check_vma=False,
    )
```
